256 devices in a mesh: group: 8 (over z), mem: 32 (over y, x, core).
Axes of the slice: x: 4, y: 4, z: 8, core: 2. Of those that a mesh axis runs over, the one named last changes fastest.
Arguments:
- memory: float32 [8, 100, 32768], P('group', None, 'mem'), may hold values from -3 to 3
- embedding: bfloat16 [128, 32768], P(None, 'mem'), may hold values from -6 to 6
- owners: int32 [8, 32768, 1], P('group', 'mem'), may hold values from 0 to 31; in each aligned block of 1024 rows (0 to 1023, 1024 to 2047, ..., all dimensions but the last counted through in order) at most 64 rows name the same one
- local_rows: int32 [8, 32768], P('group', 'mem'), may hold values from 0 to 1023
- event_slots: int32 [8, 22, 8192], P('group', None, 'mem'), may hold values from 0 to 1023
- event_ticks: int32 [8, 22, 8192], P('group', None, 'mem'), may hold values from 0 to 999
- w_self: bfloat16 [100, 228], replicated, may hold values from -0.375 to 0.375
- w_neighbour: bfloat16 [100, 228], replicated, may hold values from -0.125 to 0.125
- w_time: bfloat16 [100, 100], replicated, may hold values from -0.1875 to 0.1875
- w_link: bfloat16 [100, 200], replicated, may hold values from -0.4375 to 0.4375
- w_score: bfloat16 [100], replicated, may hold values from -0.625 to 0.625
- w_message: bfloat16 [300, 300], replicated, may hold values from -0.375 to 0.375
- w_hidden: bfloat16 [300, 100], replicated, may hold values from -0.625 to 0.625
- frequencies: float32 [100], replicated, may hold values from 0.001 to 1
- phases: float32 [100], replicated, may hold values from -3.140625 to 3.140625
Outputs:
- new_memory: bfloat16 [8, 100, 32768], P('group', None, 'mem')
- logits: bfloat16 [8, 8192], P('group', 'mem')
The draws below stay inside these ranges and needn't reach their ends.
Inputs may be any that keep to these rules, and one draw needn't show every extreme that they name: `owners`: at most 64 of the 1024 touched entries of one device name the same owner; in every draw some device names one owner exactly 64 times.
All inputs are finite; a program needn't handle non-finite values.
Results may differ from the reference program's by a relative error of at most 0.018.
Values may be sent and summed in bfloat16 or wider, within the bound.
A program may use at most 128 MiB of HBM per device.

```python
import math
import jax
import jax.numpy as jnp
import numpy as np
from jax import lax

MEMD = 100
EMBD = 128
TIMED = 100
HID = 100
LINKH = 100
NBR = 10
E_DEV = 256
TOUCH = 1024
ROWS_DEV = 1024
NODES = 32768
EVENTS = 8192
TOUCHED = 32768
CAP = 64
N_GROUP = 8
N_MEM = 32


def with_ends(result, rng, low, top_value):
    shape = result.shape
    spot = [jax.random.randint(jax.random.fold_in(rng, axis), (), 0, shape[axis]) for axis in range(len(shape))]
    result = result.at[tuple(spot)].set(low)
    longest = shape.index(max(shape))
    spot[longest] = (spot[longest] + 1) % shape[longest]
    return result.at[tuple(spot)].set(top_value)


def block_scale(own_key, extent, pieces, low, largest):
    loudness, own = 1.0, jax.random.fold_in(own_key, 6)
    for dim, blocks in pieces:
        steps = jnp.exp(jax.random.uniform(jax.random.fold_in(own, dim), (blocks,), jnp.float32, low / len(pieces), largest / len(pieces)))
        loudness = loudness * jnp.repeat(steps, extent[dim] // blocks).reshape([-1 if axis == dim else 1 for axis in range(len(extent))])
    return loudness


def routed_block(key, own, number, rows, number_of, top, reach, slope):
    order = jax.random.permutation(key, number_of)
    crowded, usual = load_shares(number_of, rows * top, reach, slope, True), load_shares(number_of, rows * top, reach, slope, False)
    places = jnp.arange(number_of)

    def named(tallies, offset_by):
        used = int((tallies > 0).sum())
        fixed = max(1, used // 4)
        passed = fixed + (places - fixed + offset_by * (used - fixed)) % max(1, number_of - fixed)
        return jnp.zeros((number_of,), jnp.int32).at[order[jnp.where(places < fixed, places, passed)]].set(jnp.asarray(tallies, jnp.int32))

    tallies = jnp.where(number % 4 == 0, named(crowded, number // 4), named(usual, number - number // 4 - 1))
    mixed = jax.random.permutation(jax.random.fold_in(own, 3), number_of)
    giver, receiver = mixed[0:number_of // 2 * 2:2], mixed[1:number_of // 2 * 2:2]
    margin = jnp.minimum(tallies[giver] - 1, reach - tallies[receiver]) // 2
    margin = jnp.where((giver == order[0]) | (receiver == order[0]) | (tallies[receiver] == 0), 0, jnp.maximum(margin, 0))
    passed = jax.random.randint(jax.random.fold_in(own, 4), (number_of // 2,), 0, 1 << 20) % (margin + 1)
    tallies = tallies.at[giver].add(-passed).at[receiver].add(passed)
    labels = jnp.searchsorted(jnp.cumsum(tallies), jnp.arange(rows * top), side="right").astype(jnp.int32)
    table = labels.reshape(top, rows).T
    table = table[jax.random.permutation(jax.random.fold_in(own, 1), rows)]
    offset_by = jax.random.randint(jax.random.fold_in(own, 2), (rows, 1), 0, top)
    return jnp.take_along_axis(table, (jnp.arange(top)[None, :] + offset_by) % top, axis=1)


def load_shares(amount, total, limit, lean, full):
    loads = [(1 << 20) // math.isqrt(rank ** lean) + 1 for rank in range(1, amount + 1)]
    largest = limit if full else min(limit, max(-(-total // amount), total * loads[0] // sum(loads)))
    least = 1 if total - largest >= amount - 1 else 0
    holding, spare = [largest] + [least] * (amount - 1), total - largest - least * (amount - 1)
    while spare > 0:
        movable = [i for i in range(1, amount) if holding[i] < largest] or [i for i in range(1, amount) if holding[i] < limit]
        pool, budget = sum([loads[i] for i in movable]), spare
        for i in movable:
            addition = min(limit - holding[i], max(1, budget * loads[i] // pool), spare)
            holding[i] = holding[i] + addition
            spare = spare - addition
    return np.array(holding)


def bell_draw(key, extent, spread, reach, pieces=(), kind=jnp.bfloat16):
    array = jax.random.normal(key, extent, jnp.float32) * spread
    if len(pieces) > 0:
        array = block_scale(key, extent, pieces, -0.22, 0.18) * array
    return jnp.clip(array, min=-reach, max=reach).astype(kind)


def setup_inputs(seed: int = 0) -> dict:
    key_list = jax.random.split(jax.random.key(seed), 16)
    memory = bell_draw(key_list[0], (N_GROUP, MEMD, NODES), 0.5, 3.0, ((0, 8), (2, 32)), jnp.float32)
    embedding = bell_draw(key_list[1], (EMBD, NODES), 1.0, 6.0, ((1, 32),))
    owners_keys = jax.random.split(jax.random.fold_in(key_list[2], 1), N_GROUP * TOUCHED // TOUCH)
    owners_turns = jax.random.permutation(jax.random.fold_in(key_list[2], 3), N_GROUP * TOUCHED // TOUCH)
    owners = jax.vmap(lambda own, number: routed_block(jax.random.fold_in(key_list[2], 2), own, number, TOUCH, N_MEM, 1, CAP, 2))(owners_keys, owners_turns).reshape((N_GROUP, TOUCHED, 1))
    local_rows = with_ends(jax.random.randint(key_list[3], (N_GROUP, TOUCHED), 0, ROWS_DEV), jax.random.fold_in(key_list[3], 1), 0, ROWS_DEV - 1).astype(jnp.int32)
    event_slots = with_ends(jax.random.randint(key_list[4], (N_GROUP, 2 + 2 * NBR, EVENTS), 0, TOUCH), jax.random.fold_in(key_list[4], 1), 0, TOUCH - 1).astype(jnp.int32)
    event_ticks = with_ends(jax.random.randint(key_list[5], (N_GROUP, 2 + 2 * NBR, EVENTS), 0, 1000), jax.random.fold_in(key_list[5], 1), 0, 999).astype(jnp.int32)
    w_self = bell_draw(key_list[6], (HID, MEMD + EMBD), (MEMD + EMBD) ** -0.5, 0.375)
    w_neighbour = bell_draw(key_list[7], (HID, MEMD + EMBD), (NBR * (MEMD + EMBD)) ** -0.5, 0.125)
    w_time = bell_draw(key_list[8], (HID, TIMED), (NBR * TIMED) ** -0.5, 0.1875)
    w_link = bell_draw(key_list[9], (LINKH, 2 * HID), (2 * HID) ** -0.5, 0.4375)
    w_score = bell_draw(key_list[10], (LINKH,), LINKH ** -0.5, 0.625)
    w_message = bell_draw(key_list[11], (3 * MEMD, 2 * MEMD + TIMED), (2 * MEMD + TIMED) ** -0.5, 0.375)
    w_hidden = bell_draw(key_list[12], (3 * MEMD, MEMD), MEMD ** -0.5, 0.625)
    frequencies = jnp.clip(jnp.exp(jax.random.uniform(key_list[13], (TIMED,), jnp.float32, math.log(0.001), math.log(1.0))), 0.001, 1.0)
    phases = jnp.clip(jax.random.uniform(key_list[14], (TIMED,), jnp.float32, -3.140625, 3.140625), -3.140625, 3.140625)
    return dict(memory=memory, embedding=embedding, owners=owners, local_rows=local_rows, event_slots=event_slots, event_ticks=event_ticks, w_self=w_self, w_neighbour=w_neighbour, w_time=w_time, w_link=w_link, w_score=w_score, w_message=w_message, w_hidden=w_hidden, frequencies=frequencies, phases=phases)


def reference(memory, embedding, owners, local_rows, event_slots, event_ticks, w_self, w_neighbour, w_time, w_link, w_score, w_message, w_hidden, frequencies, phases):
    highest = lax.Precision.HIGHEST
    handed_all = jnp.roll(memory, 1, axis=0)
    block_base = (jnp.arange(EVENTS, dtype=jnp.int32) // E_DEV) * TOUCH
    memory_list = []
    logit_list = []
    for group in range(N_GROUP):
        handed = handed_all[group]
        mem_state = handed.astype(jnp.bfloat16)
        node_ids = (owners[group, :, 0] * ROWS_DEV + local_rows[group]).astype(jnp.int32)
        fetched_state = jnp.take(mem_state, node_ids, axis=1)
        fetched_embed = jnp.take(embedding, node_ids, axis=1)
        features = jnp.concatenate([fetched_state, fetched_embed], axis=0)
        self_proj = jnp.dot(w_self, features, preferred_element_type=jnp.float32)
        neighbour_proj = jnp.dot(w_neighbour, features, preferred_element_type=jnp.float32)
        event_refs = (event_slots[group] + block_base[None, :]).astype(jnp.int32)
        tick_values = event_ticks[group].astype(jnp.float32)
        time_codes = jnp.cos(frequencies[:, None, None] * tick_values[None] + phases[:, None, None])
        neighbour_refs = event_refs[2:].reshape(2, NBR, EVENTS)
        neighbour_sum = jnp.sum(jnp.take(neighbour_proj, neighbour_refs, axis=1), axis=2)
        code_sum = jnp.sum(time_codes[:, 2:].reshape(TIMED, 2, NBR, EVENTS), axis=2)
        time_term = jnp.einsum("ht,tse->hse", w_time.astype(jnp.float32), code_sum, precision=highest)
        pre_embed = jnp.take(self_proj, event_refs[:2], axis=1) + neighbour_sum + time_term
        embeds = jax.nn.relu(pre_embed).astype(jnp.bfloat16)
        link = jax.nn.relu(jnp.einsum("lsh,hse->le", w_link.reshape(LINKH, 2, HID).astype(jnp.float32), embeds.astype(jnp.float32)))
        logit_list.append(jnp.sum(w_score.astype(jnp.float32)[:, None] * link, axis=0).astype(jnp.bfloat16))
        self_flat = event_refs[:2].reshape(-1)
        other_flat = event_refs[1::-1].reshape(-1)
        target_nodes = jnp.take(node_ids, self_flat)
        other_state = jnp.take(fetched_state, other_flat, axis=1).astype(jnp.float32)
        gap_codes = time_codes[:, :2].reshape(TIMED, 2 * EVENTS)
        payload = jnp.concatenate([other_state, gap_codes], axis=0)
        message_sum = jnp.zeros((MEMD + TIMED, NODES), jnp.float32).at[:, target_nodes].add(payload)
        message_count = jnp.zeros((NODES,), jnp.float32).at[target_nodes].add(1.0)
        own_gate = jnp.dot(w_message[:, :MEMD], mem_state, preferred_element_type=jnp.float32)
        other_gate = jnp.dot(w_message[:, MEMD:2 * MEMD].astype(jnp.float32), message_sum[:MEMD], precision=highest)
        time_gate = jnp.dot(w_message[:, 2 * MEMD:].astype(jnp.float32), message_sum[MEMD:], precision=highest)
        gates_in = (message_count[None, :] * own_gate + other_gate + time_gate) / jnp.maximum(message_count, 1.0)[None, :]
        hidden_in = jnp.dot(w_hidden, mem_state, preferred_element_type=jnp.float32)
        reset = jax.nn.sigmoid(gates_in[:MEMD] + hidden_in[:MEMD])
        update = jax.nn.sigmoid(gates_in[MEMD:2 * MEMD] + hidden_in[MEMD:2 * MEMD])
        candidate = jnp.tanh(gates_in[2 * MEMD:] + reset * hidden_in[2 * MEMD:])
        updated = (1.0 - update) * candidate + update * handed
        memory_list.append(jnp.where(message_count[None, :] > 0.0, updated, handed).astype(jnp.bfloat16))
    return jnp.stack(memory_list, axis=0), jnp.stack(logit_list, axis=0)
```

```python
import jax
import jax.numpy as jnp
from jax import lax
from jax.experimental import pallas as pl
from jax.experimental.pallas import tpu as pltpu
from jax.sharding import PartitionSpec as P

MESH = pl.DeviceIdType.MESH
F32, BF16, I32 = jnp.float32, jnp.bfloat16, jnp.int32
PEERS, CAP, LANES = 32, 64, 128
SLOTS = PEERS * CAP
TURN = 0.15915494309189535
COS = (
    0.9999999890590219,
    -19.739204499453752,
    64.93911745989001,
    -85.45013953080313,
    60.16763095037926,
    -25.96759924649648,
    6.5286581586731725,
)


def nn(a, b):
    return jnp.dot(a, b, preferred_element_type=F32)


def nt(a, b):
    return lax.dot_general(a, b, (((1,), (1,)), ((), ())), preferred_element_type=F32)


def split(x):
    high = x.astype(BF16)
    return high, (x - high.astype(F32)).astype(BF16)


def hot(mask):
    return jnp.where(mask, 1.0, 0.0).astype(BF16)


def iota(shape, dim):
    return lax.broadcasted_iota(I32, shape, dim)


def cos_turns(y):
    r = y - jnp.floor(y + 0.5)
    z = r * r
    acc = jnp.full_like(z, COS[-1])
    for c in COS[-2::-1]:
        acc = acc * z + c
    return acc


def column(row):
    return jnp.broadcast_to(row, (LANES, LANES)).T


def partner(me, d):
    out = 0
    for bit in (1, 2, 4, 8, 16):
        out = out + lax.rem(lax.div(me, bit) + lax.div(d, bit), 2) * bit
    return out


def kernel(
    mem, emb, own, rows, slots, ticks, w_self, w_neigh, w_time, w_link, w_score, w_msg, w_hid, freq, phase,
    new_mem, logits,
    hsend, hrecv, rsend, rrecv, esend, erecv, ssend, srecv, tsend, trecv, msend, mrecv,
    codes, csum, emb_t, mem_t, ask_rows, o_mat, ot_mat, g_mat, gx_mat, p_mat, c_mat, cg_mat,
    wg, wh, wp, base, other_acc, st_acc, ss_acc,
    hsem, send_sem, recv_sem,
):
    me = lax.axis_index("mem")
    group = lax.axis_index("group")
    groups = lax.axis_size("group")
    ahead = lax.rem(group + 1, groups)
    behind = lax.rem(group + groups - 1, groups)
    width, events = 100, slots.shape[2]

    barrier = pltpu.get_barrier_semaphore()
    pl.semaphore_signal(barrier, inc=1, device_id={"group": behind}, device_id_type=MESH)

    def greet(d, c):
        pl.semaphore_signal(barrier, inc=1, device_id={"mem": partner(me, d)}, device_id_type=MESH)
        return c

    lax.fori_loop(1, PEERS, greet, 0)

    def remote(phase_no, src, dst, d):
        return pltpu.make_async_remote_copy(
            src_ref=src.at[d],
            dst_ref=dst.at[d],
            send_sem=send_sem.at[phase_no, d],
            recv_sem=recv_sem.at[phase_no, d],
            device_id={"mem": partner(me, d)},
            device_id_type=MESH,
        )

    def start_all(phase_no, src, dst, low, high):
        def go(d, c):
            remote(phase_no, src, dst, d).start()
            return c

        lax.fori_loop(low, high, go, 0)

    def await_all(phase_no, src, dst, low, high):
        def go(d, c):
            remote(phase_no, src, dst, d).wait_recv()
            return c

        lax.fori_loop(low, high, go, 0)

    for j in range(8):
        block = mem[pl.ds(j, width, stride=8), :]
        hsend[0:width, j * LANES : (j + 1) * LANES] = block.astype(BF16)
    hsend[96:112, :] = jnp.where(iota((16, 1024), 0) < 4, hsend[96:112, :].astype(F32), 0.0).astype(BF16)

    own_rel = own[...] ^ me
    local = rows[...]
    upper = iota((LANES, 2 * LANES), 0)
    lane = iota((LANES, 2 * LANES), 1)
    tri = hot((lane >= LANES) | (upper < lane))
    members = [jnp.where(iota((PEERS, LANES), 0) == own_rel[r : r + 1, :], 1.0, 0.0) for r in range(8)]
    counts = nn(jnp.concatenate(members, axis=0).astype(BF16), tri)
    seen = jnp.zeros((PEERS, LANES), F32)
    ranks = []
    for r in range(8):
        part = counts[r * PEERS : (r + 1) * PEERS, :]
        ranks.append(jnp.sum(members[r] * (part[:, :LANES] + seen), axis=0, keepdims=True))
        seen = seen + part[:, LANES:]
    rank_row = jnp.concatenate(ranks, axis=1)
    own_row = jnp.concatenate([own_rel[r : r + 1, :] for r in range(8)], axis=1)
    local_row = jnp.concatenate([local[r : r + 1, :] for r in range(8)], axis=1)
    rank_int = rank_row.astype(I32)
    in_rank = (iota((LANES, 1024), 0) & (CAP - 1)) == rank_int
    local_low = local_row & 31
    high_part = jnp.where(in_rank, (local_row - local_low).astype(F32), 0.0).astype(BF16)
    low_part = jnp.where(in_rank, local_low.astype(F32), 0.0).astype(BF16)
    member_row = hot(iota((PEERS, 1024), 0) == own_row)
    request = (nt(member_row, high_part) + nt(member_row, low_part)).astype(I32)
    for d in range(PEERS):
        rsend[d] = request[d : d + 1, :]
    rrecv[0] = request[0:1, :]

    pl.semaphore_wait(barrier, PEERS)

    hand = pltpu.make_async_remote_copy(
        src_ref=hsend,
        dst_ref=hrecv,
        send_sem=hsem.at[0],
        recv_sem=hsem.at[1],
        device_id={"group": ahead},
        device_id_type=MESH,
    )
    hand.start()
    start_all(0, rsend, rrecv, 1, PEERS)

    refs = jnp.concatenate([slots[0], slots[1]], axis=1)
    sub8 = iota((16, 1024), 0)
    slot_parts = jnp.where(sub8 == 0, own_row.astype(F32), jnp.where(sub8 == 1, rank_row, 0.0)).astype(BF16)
    picked = nn(slot_parts, hot(iota((1024, 2 * events), 0) == refs))
    end_slot = (picked[0:1, :] * float(CAP) + picked[1:2, :]).astype(I32)
    other_slot = jnp.concatenate([end_slot[:, events:], end_slot[:, :events]], axis=1)

    pad = jnp.zeros((1, LANES - width), F32)
    freq_col = column(jnp.concatenate([freq[...], pad], axis=1) * TURN)[0:104, :]
    phase_col = column(jnp.concatenate([phase[...], pad], axis=1) * TURN)[0:104, :]

    def code(k):
        tick = ticks[k].astype(F32)
        return jnp.concatenate(
            [cos_turns(freq_col * tick[:, h * LANES : (h + 1) * LANES] + phase_col) for h in range(events // LANES)],
            axis=1,
        )

    sub = iota((LANES, 2 * events), 0)
    side = iota((LANES, 2 * events), 1) // events
    ends = jnp.concatenate([code(0), code(1)], axis=1)
    ends = jnp.concatenate([ends, jnp.zeros((LANES - 104, 2 * events), F32)], axis=0)
    codes[...] = jnp.where(sub < width, ends, jnp.where(sub == width + side, 1.0, 0.0)).astype(BF16)

    def time_chunk(q, c):
        at = pl.multiple_of(q * 512, 512)
        block = hot(iota((512, 2 * events), 0) + at == end_slot)
        g_mat[pl.ds(at, 512), :] = block
        sums = nt(block, codes[...]).astype(BF16)
        for i in range(8):
            tsend[q * 8 + i] = sums[i * CAP : (i + 1) * CAP, :]
        return c

    lax.fori_loop(0, 4, time_chunk, 0)
    trecv[0] = tsend[0]
    start_all(1, tsend, trecv, 1, PEERS)

    emb_t[...] = emb[...].T

    await_all(0, rsend, rrecv, 1, PEERS)
    for p in range(PEERS // 2):
        pair = jnp.where(iota((1, LANES), 1) < CAP, rrecv[2 * p], rrecv[2 * p + 1])
        ask_rows[p] = pair

    def ask_chunk(p, c):
        asked = column(ask_rows[p].astype(F32)).astype(I32)
        at = pl.multiple_of(p * LANES, LANES)
        for j in range(8):
            o_mat[pl.ds(at, LANES), j * LANES : (j + 1) * LANES] = hot(iota((LANES, LANES), 1) + j * LANES == asked)
        return c

    lax.fori_loop(0, PEERS // 2, ask_chunk, 0)

    hand.wait_recv()
    mem_t[:, 0:112] = hrecv[...].astype(F32).T.astype(BF16)
    mem_t[:, 112:128] = jnp.zeros((1024, 16), BF16)

    def serve(phase_no, table, src, dst):
        def chunk(q, c):
            at = pl.multiple_of(q * 512, 512)
            got = nn(o_mat[pl.ds(at, 512), :], table[...]).astype(BF16)
            for i in range(8):
                src[q * 8 + i] = got[i * CAP : (i + 1) * CAP, :]
            start_all(phase_no, src, dst, jnp.maximum(q * 8, 1), q * 8 + 8)
            return c

        lax.fori_loop(0, 4, chunk, 0)
        dst[0] = src[0]

    serve(2, mem_t, ssend, srecv)
    serve(3, emb_t, esend, erecv)

    wg[...] = jnp.zeros_like(wg)
    wh[...] = jnp.zeros_like(wh)
    wp[...] = jnp.zeros_like(wp)
    for gate in range(3):
        for part in range(3):
            wg[gate, part, 0:width, 0:width] = w_msg[
                gate * width : (gate + 1) * width, part * width : (part + 1) * width
            ]
        wh[gate, 0:width, 0:width] = w_hid[gate * width : (gate + 1) * width, :]
    for which, w in enumerate((w_self, w_neigh)):
        wp[which, 0, 0:width, 0:width] = w[:, 0:width]
        wp[which, 1, 0:width, :] = w[:, width:]

    for gate in range(3):
        hidden = nt(wh[gate], mem_t[...])
        own_part = nt(wg[gate, 0], mem_t[...])
        if gate < 2:
            base[gate] = hidden + own_part
        else:
            base[2] = own_part
            base[3] = hidden

    def turn_chunk(j, c):
        at = pl.multiple_of(j * LANES, LANES)
        ask = jnp.concatenate([ask_rows[p] for p in range(PEERS // 2)], axis=1)
        ot_mat[pl.ds(at, LANES), :] = hot(iota((LANES, SLOTS), 0) + at == ask)
        return c

    lax.fori_loop(0, 8, turn_chunk, 0)

    for m in range(2 * events // LANES):
        col = column(other_slot[:, m * LANES : (m + 1) * LANES].astype(F32)).astype(I32)

        def gx_chunk(j, c, col=col, m=m):
            at = pl.multiple_of(j * LANES, LANES)
            gx_mat[m * LANES : (m + 1) * LANES, pl.ds(at, LANES)] = hot(iota((LANES, LANES), 1) + at == col)
            return c

        lax.fori_loop(0, SLOTS // LANES, gx_chunk, 0)

    neighbours = (slots.shape[0] - 2) // 2

    def count_chunk(q, c):
        at = pl.multiple_of(q * CAP, CAP)
        index = iota((CAP, events), 0) + at
        for s in range(2):
            total = jnp.zeros((CAP, events), F32)
            for j in range(neighbours):
                total = total + jnp.where(index == slots[2 + s * neighbours + j], 1.0, 0.0)
            c_mat[pl.ds(at, CAP), s * events : (s + 1) * events] = total.astype(BF16)
        return c

    lax.fori_loop(0, 1024 // CAP, count_chunk, 0)
    slot_row = own_row * CAP + rank_int

    def spread_chunk(q, c):
        at = pl.multiple_of(q * 512, 512)
        p_mat[...] = hot(iota((512, 1024), 0) + at == slot_row)
        cg_mat[pl.ds(at, 512), :] = nn(p_mat[...], c_mat[...]).astype(BF16)
        return c

    lax.fori_loop(0, 4, spread_chunk, 0)

    other_acc[...] = jnp.zeros_like(other_acc)

    def other_chunk(q, c):
        await_all(2, ssend, srecv, jnp.maximum(q * 8, 1), q * 8 + 8)
        at = pl.multiple_of(q * 512, 512)
        block = srecv[pl.ds(pl.multiple_of(q * 8, 8), 8)].reshape(512, LANES)
        other_acc[...] += nn(gx_mat[:, pl.ds(at, 512)], block)
        return c

    lax.fori_loop(0, 4, other_chunk, 0)
    other_state = other_acc[...].astype(BF16)

    def state_chunk(q, c):
        at = pl.multiple_of(q * 512, 512)
        sums = nn(g_mat[pl.ds(at, 512), :], other_state).astype(BF16)
        for i in range(8):
            msend[q * 8 + i] = sums[i * CAP : (i + 1) * CAP, :]
        start_all(4, msend, mrecv, jnp.maximum(q * 8, 1), q * 8 + 8)
        return c

    lax.fori_loop(0, 4, state_chunk, 0)
    mrecv[0] = msend[0]

    for s in range(2):
        def add_code(j, total, s=s):
            return total + code(2 + s * neighbours + j)

        csum[:, s * events : (s + 1) * events] = lax.fori_loop(
            0, neighbours, add_code, jnp.zeros((104, events), F32)
        )

    await_all(1, tsend, trecv, 1, PEERS)
    st_acc[...] = nn(ot_mat[...], trecv[...].reshape(SLOTS, LANES))

    await_all(3, esend, erecv, 1, PEERS)
    state_all = srecv[...].reshape(SLOTS, LANES)
    embed_all = erecv[...].reshape(SLOTS, LANES)
    pre = jnp.zeros((112, 2 * events), F32)
    for which, table in enumerate((g_mat, cg_mat)):
        proj = nt(wp[which, 0], state_all) + nt(wp[which, 1], embed_all)
        high, low = split(proj)
        pre = pre + nn(high, table[...]) + nn(low, table[...])
    high, low = split(csum[0:width, :])
    embeds = pre[0:width, :] + nn(w_time[...], high) + nn(w_time[...], low)
    embeds = jnp.maximum(embeds, 0.0).astype(BF16)
    link = nn(w_link[:, 0:width], embeds[:, :events]) + nn(w_link[:, width:], embeds[:, events:])
    high, low = split(jnp.maximum(link, 0.0))
    score = jnp.broadcast_to(w_score[...], (16, width))
    logits[...] = (nn(score, high) + nn(score, low))[0:1, :].astype(BF16)

    ss_acc[...] = jnp.zeros_like(ss_acc)

    def sum_chunk(q, c):
        await_all(4, msend, mrecv, jnp.maximum(q * 8, 1), q * 8 + 8)
        at = pl.multiple_of(q * 512, 512)
        block = mrecv[pl.ds(pl.multiple_of(q * 8, 8), 8)].reshape(512, LANES)
        ss_acc[...] += nn(ot_mat[:, pl.ds(at, 512)], block)
        return c

    lax.fori_loop(0, 4, sum_chunk, 0)

    t_high, t_low = split(st_acc[...])
    s_high, s_low = split(ss_acc[...])
    lane16 = iota((16, LANES), 1)
    tally = hot((iota((16, LANES), 0) == 0) & ((lane16 == width) | (lane16 == width + 1)))
    count = (nt(tally, t_high) + nt(tally, t_low))[0:1, :]
    inverse = 1.0 / jnp.maximum(count, 1.0)

    def messages(gate):
        ws, wt = wg[gate, 1], wg[gate, 2]
        return (nt(ws, s_high) + nt(ws, s_low) + nt(wt, t_high) + nt(wt, t_low)) * inverse

    reset = jax.nn.sigmoid(base[0] + messages(0))
    update = jax.nn.sigmoid(base[1] + messages(1))
    candidate = jnp.tanh(base[2] + messages(2) + reset * base[3])
    handed = hrecv[...].astype(F32)
    updated = (1.0 - update) * candidate + update * handed
    new_mem[...] = jnp.where(count > 0.0, updated, handed)[0:width, :].astype(BF16)

    hand.wait_send()

    def drain(d, c):
        for phase_no, src, dst in (
            (0, rsend, rrecv), (1, tsend, trecv), (2, ssend, srecv), (3, esend, erecv), (4, msend, mrecv),
        ):
            remote(phase_no, src, dst, d).wait_send()
        return c

    lax.fori_loop(1, PEERS, drain, 0)


def local_step(
    memory, embedding, owners, local_rows, event_slots, event_ticks,
    w_self, w_neighbour, w_time, w_link, w_score, w_message, w_hidden, frequencies, phases,
):
    nodes = memory.shape[2]
    events = event_slots.shape[2]
    args = (
        memory.reshape(-1, LANES),
        embedding,
        owners.reshape(-1, LANES),
        local_rows.reshape(-1, LANES),
        event_slots.transpose(1, 0, 2),
        event_ticks.transpose(1, 0, 2),
        w_self,
        w_neighbour,
        w_time,
        w_link,
        w_score.reshape(1, -1),
        w_message,
        w_hidden,
        frequencies.reshape(1, -1),
        phases.reshape(1, -1),
    )
    vmem = pl.BlockSpec(memory_space=pltpu.VMEM)
    block = (PEERS, CAP, LANES)
    scratch = [
        pltpu.VMEM((112, nodes), BF16),
        pltpu.VMEM((112, nodes), BF16),
        pltpu.VMEM((PEERS, 1, LANES), I32),
        pltpu.VMEM((PEERS, 1, LANES), I32),
        *[pltpu.VMEM(block, BF16)] * 8,
        pltpu.VMEM((LANES, 2 * events), BF16),
        pltpu.VMEM((104, 2 * events), F32),
        pltpu.VMEM((nodes, LANES), BF16),
        pltpu.VMEM((nodes, LANES), BF16),
        pltpu.VMEM((PEERS // 2, 1, LANES), I32),
        pltpu.VMEM((SLOTS, nodes), BF16),
        pltpu.VMEM((nodes, SLOTS), BF16),
        pltpu.VMEM((SLOTS, 2 * events), BF16),
        pltpu.VMEM((2 * events, SLOTS), BF16),
        pltpu.VMEM((512, 1024), BF16),
        pltpu.VMEM((1024, 2 * events), BF16),
        pltpu.VMEM((SLOTS, 2 * events), BF16),
        pltpu.VMEM((3, 3, 112, LANES), BF16),
        pltpu.VMEM((3, 112, LANES), BF16),
        pltpu.VMEM((2, 2, 112, LANES), BF16),
        pltpu.VMEM((4, 112, nodes), F32),
        pltpu.VMEM((2 * events, LANES), F32),
        pltpu.VMEM((nodes, LANES), F32),
        pltpu.VMEM((nodes, LANES), F32),
        pltpu.SemaphoreType.DMA((2,)),
        pltpu.SemaphoreType.DMA((5, PEERS)),
        pltpu.SemaphoreType.DMA((5, PEERS)),
    ]
    new_memory, logits = pl.pallas_call(
        kernel,
        out_shape=(
            jax.ShapeDtypeStruct((memory.shape[1], nodes), BF16),
            jax.ShapeDtypeStruct((1, events), BF16),
        ),
        in_specs=[vmem] * len(args),
        out_specs=(vmem, vmem),
        scratch_shapes=scratch,
        compiler_params=pltpu.CompilerParams(
            collective_id=0, has_side_effects=True, vmem_limit_bytes=56 * 1024 * 1024
        ),
    )(*args)
    return new_memory[None], logits


def solution(mesh):
    return jax.shard_map(
        local_step,
        mesh=mesh,
        in_specs=(
            P("group", None, "mem"),
            P(None, "mem"),
            P("group", "mem", None),
            P("group", "mem"),
            P("group", None, "mem"),
            P("group", None, "mem"),
            P(),
            P(),
            P(),
            P(),
            P(),
            P(),
            P(),
            P(),
            P(),
        ),
        out_specs=(P("group", None, "mem"), P("group", "mem")),
        check_vma=False,
    )
```

```python
import jax
import jax.numpy as jnp
from jax import lax
from jax.experimental import pallas as pl
from jax.experimental.pallas import tpu as pltpu
from jax.sharding import PartitionSpec as P

MESH = pl.DeviceIdType.MESH
F32, BF16, I32, I16 = jnp.float32, jnp.bfloat16, jnp.int32, jnp.int16
PEERS, CAP, LANES = 32, 64, 128
SLOTS = PEERS * CAP
TURN = 0.15915494309189535
COS = (
    0.9999999890590219,
    -19.739204499453752,
    64.93911745989001,
    -85.45013953080313,
    60.16763095037926,
    -25.96759924649648,
    6.5286581586731725,
)


def nn(a, b):
    return jnp.dot(a, b, preferred_element_type=F32)


def nt(a, b):
    return lax.dot_general(a, b, (((1,), (1,)), ((), ())), preferred_element_type=F32)


def split(x):
    high = x.astype(BF16)
    return high, (x - high.astype(F32)).astype(BF16)


def hot(mask):
    return jnp.where(mask, 1.0, 0.0).astype(BF16)


def iota(shape, dim):
    return lax.broadcasted_iota(I32, shape, dim)


def tn(a, b):
    return lax.dot_general(a, b, (((0,), (0,)), ((), ())), preferred_element_type=F32)


def sigmoid(x):
    return 0.5 * jnp.tanh(0.5 * x) + 0.5


def hot_rows(row, count):
    shape = (16, row.shape[1])
    named = jnp.broadcast_to(row, shape).astype(I16)
    index = iota(shape, 0).astype(I16)
    one, zero = jnp.ones(shape, BF16), jnp.zeros(shape, BF16)
    return jnp.concatenate([jnp.where(index + jnp.int16(i) == named, one, zero) for i in range(0, count, 16)], axis=0)


def cos_turns(y):
    r = y - jnp.floor(y + 0.5)
    z = r * r
    acc = jnp.full_like(z, COS[-1])
    for c in COS[-2::-1]:
        acc = acc * z + c
    return acc


def column(row):
    return jnp.broadcast_to(row, (LANES, LANES)).T


def partner(me, d):
    out = 0
    for bit in (1, 2, 4, 8, 16):
        out = out + lax.rem(lax.div(me, bit) + lax.div(d, bit), 2) * bit
    return out


def kernel(
    mem, emb, own, rows, slots, ticks, w_self, w_neigh, w_time, w_link, w_score, w_msg, w_hid, freq, phase,
    new_mem, logits,
    hsend, hrecv, rsend, rrecv, esend, erecv, ssend, srecv, tsend, trecv, msend, mrecv,
    codes, csum, table, o_mat, g_mat, p_mat, c_mat,
    wg, wh, wp, base, time_part, self_acc, t_acc, s_acc,
    hsem, send_sem, recv_sem,
):
    me = lax.axis_index("mem")
    group = lax.axis_index("group")
    groups = lax.axis_size("group")
    ahead = lax.rem(group + 1, groups)
    behind = lax.rem(group + groups - 1, groups)
    width, events = 100, slots.shape[2]

    barrier = pltpu.get_barrier_semaphore()
    pl.semaphore_signal(barrier, inc=1, device_id={"group": behind}, device_id_type=MESH)

    def greet(d, c):
        pl.semaphore_signal(barrier, inc=1, device_id={"mem": partner(me, d)}, device_id_type=MESH)
        return c

    lax.fori_loop(1, PEERS, greet, 0)

    def remote(phase_no, src, dst, d):
        return pltpu.make_async_remote_copy(
            src_ref=src.at[d],
            dst_ref=dst.at[d],
            send_sem=send_sem.at[phase_no, d],
            recv_sem=recv_sem.at[phase_no, d],
            device_id={"mem": partner(me, d)},
            device_id_type=MESH,
        )

    def start_all(phase_no, src, dst, low, high):
        def go(d, c):
            remote(phase_no, src, dst, d).start()
            return c

        lax.fori_loop(low, high, go, 0)

    def await_all(phase_no, src, dst, low, high):
        def go(d, c):
            remote(phase_no, src, dst, d).wait_recv()
            return c

        lax.fori_loop(low, high, go, 0)

    for j in range(8):
        block = mem[pl.ds(j, width, stride=8), :]
        hsend[0:width, j * LANES : (j + 1) * LANES] = block.astype(BF16)
    hsend[96:112, :] = jnp.where(iota((16, 1024), 0) < 4, hsend[96:112, :].astype(F32), 0.0).astype(BF16)

    own_rel = own[...] ^ me
    local = rows[...]
    upper = iota((LANES, 2 * LANES), 0)
    lane = iota((LANES, 2 * LANES), 1)
    tri = hot((lane >= LANES) | (upper < lane))
    members = [jnp.where(iota((PEERS, LANES), 0) == own_rel[r : r + 1, :], 1.0, 0.0) for r in range(8)]
    counts = nn(jnp.concatenate(members, axis=0).astype(BF16), tri)
    seen = jnp.zeros((PEERS, LANES), F32)
    ranks = []
    for r in range(8):
        part = counts[r * PEERS : (r + 1) * PEERS, :]
        ranks.append(jnp.sum(members[r] * (part[:, :LANES] + seen), axis=0, keepdims=True))
        seen = seen + part[:, LANES:]
    rank_row = jnp.concatenate(ranks, axis=1)
    own_row = jnp.concatenate([own_rel[r : r + 1, :] for r in range(8)], axis=1)
    local_row = jnp.concatenate([local[r : r + 1, :] for r in range(8)], axis=1)
    rank_int = rank_row.astype(I32)
    in_rank = (iota((LANES, 1024), 0) & (CAP - 1)) == rank_int
    local_low = local_row & 31
    high_part = jnp.where(in_rank, (local_row - local_low).astype(F32), 0.0).astype(BF16)
    low_part = jnp.where(in_rank, local_low.astype(F32), 0.0).astype(BF16)
    member_row = hot_rows(own_row, PEERS)
    request = (nt(member_row, high_part) + nt(member_row, low_part)).astype(I32)
    for d in range(PEERS):
        rsend[d] = request[d : d + 1, :]
    rrecv[0] = request[0:1, :]

    refs = jnp.concatenate([slots[0], slots[1]], axis=1)
    sub8 = iota((16, 1024), 0)
    slot_parts = jnp.where(sub8 == 0, own_row.astype(F32), jnp.where(sub8 == 1, rank_row, 0.0)).astype(BF16)
    picked = nn(slot_parts, hot_rows(refs, 1024))
    end_slot = (picked[0:1, :] * float(CAP) + picked[1:2, :]).astype(I32)
    g_mat[...] = hot_rows(end_slot, SLOTS)

    pad = jnp.zeros((1, LANES - width), F32)
    freq_col = column(jnp.concatenate([freq[...], pad], axis=1) * TURN)[0:104, :]
    phase_col = column(jnp.concatenate([phase[...], pad], axis=1) * TURN)[0:104, :]

    def code(k):
        tick = ticks[k].astype(F32)
        return jnp.concatenate(
            [cos_turns(freq_col * tick[:, h * LANES : (h + 1) * LANES] + phase_col) for h in range(events // LANES)],
            axis=1,
        )

    sub = iota((LANES, 2 * events), 0)
    side = iota((LANES, 2 * events), 1) // events
    ends = jnp.concatenate([code(0), code(1)], axis=1)
    ends = jnp.concatenate([ends, jnp.zeros((LANES - 104, 2 * events), F32)], axis=0)
    codes[...] = jnp.where(sub < width, ends, jnp.where(sub == width + side, 1.0, 0.0)).astype(BF16)

    sums = nt(g_mat[...], codes[...]).astype(BF16)
    for d in range(PEERS):
        tsend[d] = sums[d * CAP : (d + 1) * CAP, :]
    trecv[0] = tsend[0]
    table[:, LANES:] = emb[...].T

    pl.semaphore_wait(barrier, PEERS)

    hand = pltpu.make_async_remote_copy(
        src_ref=hsend,
        dst_ref=hrecv,
        send_sem=hsem.at[0],
        recv_sem=hsem.at[1],
        device_id={"group": ahead},
        device_id_type=MESH,
    )
    hand.start()
    start_all(0, rsend, rrecv, 1, PEERS)
    start_all(1, tsend, trecv, 1, PEERS)

    wg[...] = jnp.zeros_like(wg)
    wh[...] = jnp.zeros_like(wh)
    wp[...] = jnp.zeros_like(wp)
    for gate in range(3):
        for part in range(3):
            wg[part, gate * 112 : gate * 112 + width, 0:width] = w_msg[
                gate * width : (gate + 1) * width, part * width : (part + 1) * width
            ]
        wh[gate * 112 : gate * 112 + width, 0:width] = w_hid[gate * width : (gate + 1) * width, :]
    tally_lane = iota((16, LANES), 1)
    tally = (iota((16, LANES), 0) == 0) & ((tally_lane == width) | (tally_lane == width + 1))
    wg[2, 336:352, :] = hot(tally)
    for which, w in enumerate((w_self, w_neigh)):
        wp[which, 0:width, 0:width] = w[:, 0:width]
        wp[which, 0:width, LANES:] = w[:, width:]

    neighbours = (slots.shape[0] - 2) // 2
    one, zero = jnp.ones((16, 2 * events), BF16), jnp.zeros((16, 2 * events), BF16)
    index16 = iota((16, 2 * events), 0).astype(I16)
    near = [
        jnp.broadcast_to(jnp.concatenate([slots[2 + j], slots[2 + neighbours + j]], axis=1), one.shape).astype(I16)
        for j in range(neighbours)
    ]
    for q in range(64):
        total = zero
        index = index16 + jnp.int16(q * 16)
        for j in range(neighbours):
            total = total + jnp.where(index == near[j], one, zero)
        c_mat[q * 16 : (q + 1) * 16, :] = total
    p_mat[...] = hot_rows(own_row * CAP + rank_int, SLOTS)

    for s in range(2):
        def add_code(j, total, s=s):
            return total + code(2 + s * neighbours + j)

        csum[:, s * events : (s + 1) * events] = lax.fori_loop(
            0, neighbours, add_code, jnp.zeros((104, events), F32)
        )

    await_all(0, rsend, rrecv, 1, PEERS)
    for p in range(PEERS // 2):
        pair = jnp.where(iota((1, LANES), 1) < CAP, rrecv[2 * p], rrecv[2 * p + 1])
        asked = column(pair.astype(F32)).astype(I32).astype(I16)
        for j in range(8):
            index = (iota((LANES, LANES), 1) + j * LANES).astype(I16)
            o_mat[p * LANES : (p + 1) * LANES, j * LANES : (j + 1) * LANES] = jnp.where(
                index == asked, jnp.ones((LANES, LANES), BF16), jnp.zeros((LANES, LANES), BF16)
            )
    hand.wait_recv()
    table[:, 0:112] = hrecv[...].T
    table[:, 112:128] = jnp.zeros((1024, 16), BF16)
    for q in range(4):
        got = nn(o_mat[q * 512 : (q + 1) * 512, :], table[...]).astype(BF16)
        for i in range(8):
            ssend[q * 8 + i] = got[i * CAP : (i + 1) * CAP, :LANES]
            esend[q * 8 + i] = got[i * CAP : (i + 1) * CAP, LANES:]
        start_all(2, ssend, srecv, max(q * 8, 1), q * 8 + 8)
    start_all(3, esend, erecv, 1, PEERS)
    srecv[0] = ssend[0]
    erecv[0] = esend[0]

    base[0:336, :] = nn(wg[0, 0:336, 0:112], hrecv[...])
    hidden = nn(wh[...], hrecv[...])
    base[0:224, :] = base[0:224, :] + hidden[0:224, :]
    base[336:448, :] = hidden[224:336, :]

    for q in range(4):
        await_all(2, ssend, srecv, max(q * 8, 1), q * 8 + 8)
        block = srecv[q * 8 : (q + 1) * 8].reshape(512, LANES)
        part = tn(block, g_mat[q * 512 : (q + 1) * 512, :])
        self_acc[...] = part if q == 0 else self_acc[...] + part
    self_state = self_acc[...].astype(BF16)
    other_state = jnp.concatenate([self_state[:, events:], self_state[:, :events]], axis=1)
    for q in range(4):
        sums = nt(g_mat[q * 512 : (q + 1) * 512, :], other_state).astype(BF16)
        for i in range(8):
            msend[q * 8 + i] = sums[i * CAP : (i + 1) * CAP, :]
        start_all(4, msend, mrecv, max(q * 8, 1), q * 8 + 8)
    mrecv[0] = msend[0]

    await_all(1, tsend, trecv, 1, PEERS)
    t_acc[...] = tn(trecv[...].reshape(SLOTS, LANES), o_mat[...]).astype(BF16)
    time_part[...] = nn(wg[2], t_acc[...])

    await_all(3, esend, erecv, 1, PEERS)
    embed_all = erecv[...].reshape(SLOTS, LANES)
    fetched_state = tn(srecv[...].reshape(SLOTS, LANES), p_mat[...]).astype(BF16)
    fetched_embed = tn(embed_all, p_mat[...]).astype(BF16)
    near_state = nn(fetched_state, c_mat[...])
    near_embed = nn(fetched_embed, c_mat[...])
    self_embed = tn(embed_all, g_mat[...]).astype(BF16)
    pre = nn(wp[0], jnp.concatenate([self_state, self_embed], axis=0))
    for half in split(jnp.concatenate([near_state, near_embed], axis=0)):
        pre = pre + nn(wp[1], half)
    high, low = split(csum[0:width, :])
    embeds = pre[0:width, :] + nn(w_time[...], high) + nn(w_time[...], low)
    embeds = jnp.maximum(embeds, 0.0).astype(BF16)
    link = tn(w_link[0:width, :], embeds[:, :events]) + tn(w_link[width:, :], embeds[:, events:])
    high, low = split(jnp.maximum(link, 0.0))
    score = jnp.broadcast_to(w_score[...], (16, width))
    logits[...] = (nn(score, high) + nn(score, low))[0:1, :].astype(BF16)

    for q in range(4):
        await_all(4, msend, mrecv, max(q * 8, 1), q * 8 + 8)
        block = mrecv[q * 8 : (q + 1) * 8].reshape(512, LANES)
        part = tn(block, o_mat[q * 512 : (q + 1) * 512, :])
        s_acc[...] = part if q == 0 else s_acc[...] + part

    for j in range(4):
        at = slice(j * 256, (j + 1) * 256)
        count = time_part[336:337, at]
        inverse = 1.0 / jnp.maximum(count, 1.0)
        total = (nn(wg[1, 0:336, :], s_acc[:, at].astype(BF16)) + time_part[0:336, at]) * inverse + base[0:336, at]
        reset = sigmoid(total[0:112])
        update = sigmoid(total[112:224])
        candidate = jnp.tanh(total[224:336] + reset * base[336:448, at])
        handed = hrecv[:, at].astype(F32)
        updated = candidate + update * (handed - candidate)
        new_mem[:, at] = jnp.where(count > 0.0, updated, handed)[0:width, :].astype(BF16)

    hand.wait_send()

    def drain(d, c):
        for phase_no, src, dst in (
            (0, rsend, rrecv), (1, tsend, trecv), (2, ssend, srecv), (3, esend, erecv), (4, msend, mrecv),
        ):
            remote(phase_no, src, dst, d).wait_send()
        return c

    lax.fori_loop(1, PEERS, drain, 0)


def local_step(
    memory, embedding, owners, local_rows, event_slots, event_ticks,
    w_self, w_neighbour, w_time, w_link, w_score, w_message, w_hidden, frequencies, phases,
):
    nodes = memory.shape[2]
    events = event_slots.shape[2]
    args = (
        memory.reshape(-1, LANES),
        embedding,
        owners.reshape(-1, LANES),
        local_rows.reshape(-1, LANES),
        event_slots.transpose(1, 0, 2),
        event_ticks.transpose(1, 0, 2),
        w_self,
        w_neighbour,
        w_time,
        w_link.T,
        w_score.reshape(1, -1),
        w_message,
        w_hidden,
        frequencies.reshape(1, -1),
        phases.reshape(1, -1),
    )
    vmem = pl.BlockSpec(memory_space=pltpu.VMEM)
    block = (PEERS, CAP, LANES)
    scratch = [
        pltpu.VMEM((112, nodes), BF16),
        pltpu.VMEM((112, nodes), BF16),
        pltpu.VMEM((PEERS, 1, LANES), I32),
        pltpu.VMEM((PEERS, 1, LANES), I32),
        *[pltpu.VMEM(block, BF16)] * 8,
        pltpu.VMEM((LANES, 2 * events), BF16),
        pltpu.VMEM((104, 2 * events), F32),
        pltpu.VMEM((nodes, 2 * LANES), BF16),
        pltpu.VMEM((SLOTS, nodes), BF16),
        pltpu.VMEM((SLOTS, 2 * events), BF16),
        pltpu.VMEM((SLOTS, nodes), BF16),
        pltpu.VMEM((nodes, 2 * events), BF16),
        pltpu.VMEM((3, 352, LANES), BF16),
        pltpu.VMEM((336, 112), BF16),
        pltpu.VMEM((2, 112, 2 * LANES), BF16),
        pltpu.VMEM((448, nodes), F32),
        pltpu.VMEM((352, nodes), F32),
        pltpu.VMEM((LANES, 2 * events), F32),
        pltpu.VMEM((LANES, nodes), BF16),
        pltpu.VMEM((LANES, nodes), F32),
        pltpu.SemaphoreType.DMA((2,)),
        pltpu.SemaphoreType.DMA((5, PEERS)),
        pltpu.SemaphoreType.DMA((5, PEERS)),
    ]
    new_memory, logits = pl.pallas_call(
        kernel,
        out_shape=(
            jax.ShapeDtypeStruct((memory.shape[1], nodes), BF16),
            jax.ShapeDtypeStruct((1, events), BF16),
        ),
        in_specs=[vmem] * len(args),
        out_specs=(vmem, vmem),
        scratch_shapes=scratch,
        compiler_params=pltpu.CompilerParams(
            collective_id=0, has_side_effects=True, vmem_limit_bytes=56 * 1024 * 1024
        ),
    )(*args)
    return new_memory[None], logits


def solution(mesh):
    return jax.shard_map(
        local_step,
        mesh=mesh,
        in_specs=(
            P("group", None, "mem"),
            P(None, "mem"),
            P("group", "mem", None),
            P("group", "mem"),
            P("group", None, "mem"),
            P("group", None, "mem"),
            P(),
            P(),
            P(),
            P(),
            P(),
            P(),
            P(),
            P(),
            P(),
        ),
        out_specs=(P("group", None, "mem"), P("group", "mem")),
        check_vma=False,
    )
```

```python
import jax
import jax.numpy as jnp
from jax import lax
from jax.experimental import pallas as pl
from jax.experimental.pallas import tpu as pltpu
from jax.sharding import PartitionSpec as P

MESH = pl.DeviceIdType.MESH
F32, BF16, I32, I16 = jnp.float32, jnp.bfloat16, jnp.int32, jnp.int16
PEERS, CAP, LANES = 32, 64, 128
FIRST = 32
SLOTS = PEERS * CAP
TURN = 0.15915494309189535
COS = (
    0.9999999890590219,
    -19.739204499453752,
    64.93911745989001,
    -85.45013953080313,
    60.16763095037926,
    -25.96759924649648,
    6.5286581586731725,
)


def nn(a, b):
    return jnp.dot(a, b, preferred_element_type=F32)


def nt(a, b):
    return lax.dot_general(a, b, (((1,), (1,)), ((), ())), preferred_element_type=F32)


def split(x):
    high = x.astype(BF16)
    return high, (x - high.astype(F32)).astype(BF16)


def hot(mask):
    return jnp.where(mask, 1.0, 0.0).astype(BF16)


def iota(shape, dim):
    return lax.broadcasted_iota(I32, shape, dim)


def tn(a, b):
    return lax.dot_general(a, b, (((0,), (0,)), ((), ())), preferred_element_type=F32)


def sigmoid(x):
    return 0.5 * jnp.tanh(0.5 * x) + 0.5


def hot_rows(row, count):
    shape = (16, row.shape[1])
    named = jnp.broadcast_to(row, shape).astype(I16)
    index = iota(shape, 0).astype(I16)
    one, zero = jnp.ones(shape, BF16), jnp.zeros(shape, BF16)
    return jnp.concatenate([jnp.where(index + jnp.int16(i) == named, one, zero) for i in range(0, count, 16)], axis=0)


def cos_turns(y):
    r = y - jnp.floor(y + 0.5)
    z = r * r
    acc = jnp.full_like(z, COS[-1])
    for c in COS[-2::-1]:
        acc = acc * z + c
    return acc


def column(row):
    return jnp.broadcast_to(row, (LANES, LANES)).T


def partner(me, d):
    out = 0
    for bit in (1, 2, 4, 8, 16):
        out = out + lax.rem(lax.div(me, bit) + lax.div(d, bit), 2) * bit
    return out


def kernel(
    mem_in, emb_in, own, rows, slots, ticks, w_self_in, w_neigh_in, w_time, w_link, w_score, w_msg_in, w_hid_in,
    freq, phase,
    new_mem, logits,
    mem, emb, w_self, w_neigh, w_msg, w_hid,
    hsend, hrecv, rsend, rrecv, esend, erecv, ssend, srecv, tsend, trecv, msend, mrecv,
    codes, csum, o_mat, g_mat, p_mat, c_mat,
    wg, wh, wp, base, time_part, self_acc, t_acc, s_acc,
    in_sem, hsem, column_sem, send_sem, recv_sem,
):
    me = lax.axis_index("mem")
    group = lax.axis_index("group")
    groups = lax.axis_size("group")
    ahead = lax.rem(group + 1, groups)
    behind = lax.rem(group + groups - 1, groups)
    width, events = 100, slots.shape[2]

    barrier = pltpu.get_barrier_semaphore()
    columns = (8, 16, 24)
    pl.semaphore_signal(barrier, inc=1, device_id={"group": behind}, device_id_type=MESH)
    for d in (1, 2, 3, 4, 5, 6, 7, *columns):
        pl.semaphore_signal(barrier, inc=1, device_id={"mem": partner(me, d)}, device_id_type=MESH)
    loads = [
        pltpu.make_async_copy(src, dst, in_sem.at[i])
        for i, (src, dst) in enumerate(
            (
                (mem_in, mem), (emb_in, emb), (w_self_in, w_self), (w_neigh_in, w_neigh), (w_msg_in, w_msg),
                (w_hid_in, w_hid),
            )
        )
    ]
    for load in loads:
        load.start()

    def remote(phase_no, src, dst, d):
        return pltpu.make_async_remote_copy(
            src_ref=src.at[d],
            dst_ref=dst.at[d],
            send_sem=send_sem.at[phase_no, d],
            recv_sem=recv_sem.at[phase_no, d],
            device_id={"mem": partner(me, d)},
            device_id_type=MESH,
        )

    def start_all(phase_no, src, dst, low, high):
        def go(d, c):
            remote(phase_no, src, dst, d).start()
            return c

        lax.fori_loop(low, high, go, 0)

    def await_all(phase_no, src, dst, low, high):
        def go(d, c):
            remote(phase_no, src, dst, d).wait_recv()
            return c

        lax.fori_loop(low, high, go, 0)

    loads[0].wait()
    for j in range(8):
        block = mem[pl.ds(j, width, stride=8), :]
        hsend[0:width, j * LANES : (j + 1) * LANES] = block.astype(BF16)
    hsend[96:112, :] = jnp.where(iota((16, 1024), 0) < 4, hsend[96:112, :].astype(F32), 0.0).astype(BF16)

    own_rel = own[...] ^ me
    local = rows[...]
    upper = iota((LANES, 2 * LANES), 0)
    lane = iota((LANES, 2 * LANES), 1)
    tri = hot((lane >= LANES) | (upper < lane))
    members = [jnp.where(iota((PEERS, LANES), 0) == own_rel[r : r + 1, :], 1.0, 0.0) for r in range(8)]
    counts = nn(jnp.concatenate(members, axis=0).astype(BF16), tri)
    seen = jnp.zeros((PEERS, LANES), F32)
    ranks = []
    for r in range(8):
        part = counts[r * PEERS : (r + 1) * PEERS, :]
        ranks.append(jnp.sum(members[r] * (part[:, :LANES] + seen), axis=0, keepdims=True))
        seen = seen + part[:, LANES:]
    rank_row = jnp.concatenate(ranks, axis=1)
    own_row = jnp.concatenate([own_rel[r : r + 1, :] for r in range(8)], axis=1)
    local_row = jnp.concatenate([local[r : r + 1, :] for r in range(8)], axis=1)
    rank_int = rank_row.astype(I32)
    in_rank = (iota((LANES, 1024), 0) & (CAP - 1)) == rank_int
    local_low = local_row & 31
    high_part = jnp.where(in_rank, (local_row - local_low).astype(F32), 0.0).astype(BF16)
    low_part = jnp.where(in_rank, local_low.astype(F32), 0.0).astype(BF16)
    member_row = hot_rows(own_row, PEERS)
    request = (nt(member_row, high_part) + nt(member_row, low_part)).astype(I32)
    for d in range(PEERS):
        rsend[d] = request[d : d + 1, :]
    rrecv[0] = request[0:1, :]

    pl.semaphore_wait(barrier, 11)
    hand = pltpu.make_async_remote_copy(
        src_ref=hsend,
        dst_ref=hrecv.at[0:112],
        send_sem=hsem.at[0],
        recv_sem=hsem.at[1],
        device_id={"group": ahead},
        device_id_type=MESH,
    )
    hand.start()
    for d in columns:
        pl.semaphore_signal(column_sem, inc=1, device_id={"mem": partner(me, d)}, device_id_type=MESH)
    pl.semaphore_wait(column_sem, 3)
    start_all(0, rsend, rrecv, 1, PEERS)

    refs = jnp.concatenate([slots[0], slots[1]], axis=1)
    sub8 = iota((16, 1024), 0)
    slot_parts = jnp.where(sub8 == 0, own_row.astype(F32), jnp.where(sub8 == 1, rank_row, 0.0)).astype(BF16)
    picked = nn(slot_parts, hot_rows(refs, 1024))
    end_slot = (picked[0:1, :] * float(CAP) + picked[1:2, :]).astype(I32)
    g_mat[...] = hot_rows(end_slot, SLOTS)

    pad = jnp.zeros((1, LANES - width), F32)
    freq_col = column(jnp.concatenate([freq[...], pad], axis=1) * TURN)[0:104, :]
    phase_col = column(jnp.concatenate([phase[...], pad], axis=1) * TURN)[0:104, :]

    def code(k):
        tick = ticks[k].astype(F32)
        return jnp.concatenate(
            [cos_turns(freq_col * tick[:, h * LANES : (h + 1) * LANES] + phase_col) for h in range(events // LANES)],
            axis=1,
        )

    sub = iota((LANES, 2 * events), 0)
    side = iota((LANES, 2 * events), 1) // events
    ends = jnp.concatenate([code(0), code(1)], axis=1)
    ends = jnp.concatenate([ends, jnp.zeros((LANES - 104, 2 * events), F32)], axis=0)
    codes[...] = jnp.where(sub < width, ends, jnp.where(sub == width + side, 1.0, 0.0)).astype(BF16)

    sums = nt(g_mat[...], codes[...]).astype(BF16)
    for d in range(PEERS):
        tsend[d] = sums[d * CAP : (d + 1) * CAP, :]
    trecv[0] = tsend[0]
    start_all(1, tsend, trecv, 1, PEERS)

    await_all(0, rsend, rrecv, 1, PEERS)
    for p in range(PEERS // 2):
        pair = jnp.where(iota((1, LANES), 1) < CAP, rrecv[2 * p], rrecv[2 * p + 1])
        asked = column(pair.astype(F32)).astype(I32).astype(I16)
        for j in range(8):
            index = (iota((LANES, LANES), 1) + j * LANES).astype(I16)
            o_mat[p * LANES : (p + 1) * LANES, j * LANES : (j + 1) * LANES] = jnp.where(
                index == asked, jnp.ones((LANES, LANES), BF16), jnp.zeros((LANES, LANES), BF16)
            )
    def serve(rows_of, src, phase_no=None, dst=None):
        for q in range(4):
            got = nt(o_mat[q * 512 : (q + 1) * 512, :], rows_of[...]).astype(BF16)
            for i in range(8):
                src[q * 8 + i] = got[i * CAP : (i + 1) * CAP, :]
            if dst is not None:
                start_all(phase_no, src, dst, max(q * 8, 1), q * 8 + 8)

    hand.wait_recv()
    hrecv[112:128, :] = jnp.zeros((16, 1024), BF16)
    serve(hrecv, ssend, 2, srecv)
    srecv[0] = ssend[0]
    loads[1].wait()
    serve(emb, esend)
    erecv[0] = esend[0]
    start_all(3, esend, erecv, 1, FIRST)

    for load in loads[2:]:
        load.wait()
    wg[...] = jnp.zeros_like(wg)
    wh[...] = jnp.zeros_like(wh)
    wp[...] = jnp.zeros_like(wp)
    for gate in range(3):
        for part in range(3):
            wg[part, gate * 112 : gate * 112 + width, 0:width] = w_msg[
                gate * width : (gate + 1) * width, part * width : (part + 1) * width
            ]
        wh[gate * 112 : gate * 112 + width, 0:width] = w_hid[gate * width : (gate + 1) * width, :]
    tally_lane = iota((16, LANES), 1)
    tally = (iota((16, LANES), 0) == 0) & ((tally_lane == width) | (tally_lane == width + 1))
    wg[2, 336:352, :] = hot(tally)
    for which, w in enumerate((w_self, w_neigh)):
        wp[which, 0:width, 0:width] = w[:, 0:width]
        wp[which, 0:width, LANES:] = w[:, width:]

    neighbours = (slots.shape[0] - 2) // 2
    one, zero = jnp.ones((16, 2 * events), BF16), jnp.zeros((16, 2 * events), BF16)
    index16 = iota((16, 2 * events), 0).astype(I16)
    near = [
        jnp.broadcast_to(jnp.concatenate([slots[2 + j], slots[2 + neighbours + j]], axis=1), one.shape).astype(I16)
        for j in range(neighbours)
    ]
    for q in range(64):
        total = zero
        index = index16 + jnp.int16(q * 16)
        for j in range(neighbours):
            total = total + jnp.where(index == near[j], one, zero)
        c_mat[q * 16 : (q + 1) * 16, :] = total
    p_mat[...] = hot_rows(own_row * CAP + rank_int, SLOTS)

    for s in range(2):
        def add_code(j, total, s=s):
            return total + code(2 + s * neighbours + j)

        csum[:, s * events : (s + 1) * events] = lax.fori_loop(
            0, neighbours, add_code, jnp.zeros((104, events), F32)
        )

    base[0:336, :] = nn(wg[0, 0:336, 0:112], hrecv[0:112, :])
    hidden = nn(wh[...], hrecv[0:112, :])
    base[0:224, :] = base[0:224, :] + hidden[0:224, :]
    base[336:448, :] = hidden[224:336, :]

    for q in range(4):
        await_all(2, ssend, srecv, max(q * 8, 1), q * 8 + 8)
        block = srecv[q * 8 : (q + 1) * 8].reshape(512, LANES)
        part = tn(block, g_mat[q * 512 : (q + 1) * 512, :])
        self_acc[...] = part if q == 0 else self_acc[...] + part
    self_state = self_acc[...].astype(BF16)
    other_state = jnp.concatenate([self_state[:, events:], self_state[:, :events]], axis=1)
    for q in range(4):
        sums = nt(g_mat[q * 512 : (q + 1) * 512, :], other_state).astype(BF16)
        for i in range(8):
            msend[q * 8 + i] = sums[i * CAP : (i + 1) * CAP, :]
        start_all(4, msend, mrecv, max(q * 8, 1), q * 8 + 8)
    start_all(3, esend, erecv, FIRST, PEERS)
    mrecv[0] = msend[0]

    await_all(1, tsend, trecv, 1, PEERS)
    t_acc[...] = tn(trecv[...].reshape(SLOTS, LANES), o_mat[...]).astype(BF16)
    time_part[...] = nn(wg[2], t_acc[...])

    await_all(3, esend, erecv, 1, PEERS)
    embed_all = erecv[...].reshape(SLOTS, LANES)
    fetched_state = tn(srecv[...].reshape(SLOTS, LANES), p_mat[...]).astype(BF16)
    fetched_embed = tn(embed_all, p_mat[...]).astype(BF16)
    near_state = nn(fetched_state, c_mat[...])
    near_embed = nn(fetched_embed, c_mat[...])
    self_embed = tn(embed_all, g_mat[...]).astype(BF16)
    pre = nn(wp[0], jnp.concatenate([self_state, self_embed], axis=0))
    for half in split(jnp.concatenate([near_state, near_embed], axis=0)):
        pre = pre + nn(wp[1], half)
    high, low = split(csum[0:width, :])
    embeds = pre[0:width, :] + nn(w_time[...], high) + nn(w_time[...], low)
    embeds = jnp.maximum(embeds, 0.0).astype(BF16)
    link = tn(w_link[0:width, :], embeds[:, :events]) + tn(w_link[width:, :], embeds[:, events:])
    high, low = split(jnp.maximum(link, 0.0))
    score = jnp.broadcast_to(w_score[...], (16, width))
    logits[...] = (nn(score, high) + nn(score, low))[0:1, :].astype(BF16)

    for q in range(4):
        await_all(4, msend, mrecv, max(q * 8, 1), q * 8 + 8)
        block = mrecv[q * 8 : (q + 1) * 8].reshape(512, LANES)
        part = tn(block, o_mat[q * 512 : (q + 1) * 512, :])
        s_acc[...] = part if q == 0 else s_acc[...] + part

    for j in range(4):
        at = slice(j * 256, (j + 1) * 256)
        count = time_part[336:337, at]
        inverse = 1.0 / jnp.maximum(count, 1.0)
        total = (nn(wg[1, 0:336, :], s_acc[:, at].astype(BF16)) + time_part[0:336, at]) * inverse + base[0:336, at]
        reset = sigmoid(total[0:112])
        update = sigmoid(total[112:224])
        candidate = jnp.tanh(total[224:336] + reset * base[336:448, at])
        handed = hrecv[0:112, at].astype(F32)
        updated = candidate + update * (handed - candidate)
        new_mem[:, at] = jnp.where(count > 0.0, updated, handed)[0:width, :].astype(BF16)

    hand.wait_send()

    def drain(d, c):
        for phase_no, src, dst in (
            (0, rsend, rrecv), (1, tsend, trecv), (2, ssend, srecv), (3, esend, erecv), (4, msend, mrecv),
        ):
            remote(phase_no, src, dst, d).wait_send()
        return c

    lax.fori_loop(1, PEERS, drain, 0)


def hand_out(new_mem_in, logits_in, new_mem, logits):
    new_mem[...] = new_mem_in[...]
    logits[...] = logits_in[...]


def local_step(
    memory, embedding, owners, local_rows, event_slots, event_ticks,
    w_self, w_neighbour, w_time, w_link, w_score, w_message, w_hidden, frequencies, phases,
):
    nodes = memory.shape[2]
    events = event_slots.shape[2]
    args = (
        memory.reshape(-1, LANES),
        embedding,
        owners.reshape(-1, LANES),
        local_rows.reshape(-1, LANES),
        event_slots.transpose(1, 0, 2),
        event_ticks.transpose(1, 0, 2),
        w_self,
        w_neighbour,
        w_time,
        w_link.T,
        w_score.reshape(1, -1),
        w_message,
        w_hidden,
        frequencies.reshape(1, -1),
        phases.reshape(1, -1),
    )
    vmem = pl.BlockSpec(memory_space=pltpu.VMEM)
    hbm = pl.BlockSpec(memory_space=pl.ANY)
    block = (PEERS, CAP, LANES)
    scratch = [
        *[pltpu.VMEM(args[i].shape, args[i].dtype) for i in (0, 1, 6, 7, 11, 12)],
        pltpu.VMEM((112, nodes), BF16),
        pltpu.VMEM((LANES, nodes), BF16),
        pltpu.VMEM((PEERS, 1, LANES), I32),
        pltpu.VMEM((PEERS, 1, LANES), I32),
        *[pltpu.VMEM(block, BF16)] * 8,
        pltpu.VMEM((LANES, 2 * events), BF16),
        pltpu.VMEM((104, 2 * events), F32),
        pltpu.VMEM((SLOTS, nodes), BF16),
        pltpu.VMEM((SLOTS, 2 * events), BF16),
        pltpu.VMEM((SLOTS, nodes), BF16),
        pltpu.VMEM((nodes, 2 * events), BF16),
        pltpu.VMEM((3, 352, LANES), BF16),
        pltpu.VMEM((336, 112), BF16),
        pltpu.VMEM((2, 112, 2 * LANES), BF16),
        pltpu.VMEM((448, nodes), F32),
        pltpu.VMEM((352, nodes), F32),
        pltpu.VMEM((LANES, 2 * events), F32),
        pltpu.VMEM((LANES, nodes), BF16),
        pltpu.VMEM((LANES, nodes), F32),
        pltpu.SemaphoreType.DMA((6,)),
        pltpu.SemaphoreType.DMA((2,)),
        pltpu.SemaphoreType.REGULAR,
        pltpu.SemaphoreType.DMA((5, PEERS)),
        pltpu.SemaphoreType.DMA((5, PEERS)),
    ]
    new_memory, logits = pl.pallas_call(
        kernel,
        out_shape=(
            jax.ShapeDtypeStruct((memory.shape[1], nodes), BF16),
            jax.ShapeDtypeStruct((1, events), BF16),
        ),
        in_specs=[hbm if i in (0, 1, 6, 7, 11, 12) else vmem for i in range(len(args))],
        out_specs=(vmem, vmem),
        scratch_shapes=scratch,
        compiler_params=pltpu.CompilerParams(
            collective_id=0, has_side_effects=True, vmem_limit_bytes=56 * 1024 * 1024
        ),
    )(*args)
    new_memory, logits = pl.pallas_call(
        hand_out,
        out_shape=(
            jax.ShapeDtypeStruct((memory.shape[1], nodes), BF16),
            jax.ShapeDtypeStruct((1, events), BF16),
        ),
        in_specs=[vmem, vmem],
        out_specs=(vmem, vmem),
    )(new_memory, logits)
    return new_memory[None], logits


def solution(mesh):
    return jax.shard_map(
        local_step,
        mesh=mesh,
        in_specs=(
            P("group", None, "mem"),
            P(None, "mem"),
            P("group", "mem", None),
            P("group", "mem"),
            P("group", None, "mem"),
            P("group", None, "mem"),
            P(),
            P(),
            P(),
            P(),
            P(),
            P(),
            P(),
            P(),
            P(),
        ),
        out_specs=(P("group", None, "mem"), P("group", "mem")),
        check_vma=False,
    )
```

```python
import jax
import jax.numpy as jnp
from jax import lax
from jax.experimental import pallas as pl
from jax.experimental.pallas import tpu as pltpu
from jax.sharding import PartitionSpec as P

MESH = pl.DeviceIdType.MESH
F32, BF16, I32, I16 = jnp.float32, jnp.bfloat16, jnp.int32, jnp.int16
PEERS, CAP, LANES = 32, 64, 128
Y_ORDER = (2, 1, 3, 0)
FAR_FIRST = [8 * y + x for y in Y_ORDER for x in (4, 5, 2, 3, 6, 7, 0, 1) if 8 * y + x > 0]
SLOTS = PEERS * CAP
TURN = 0.15915494309189535
COS = (
    0.9999999890590219,
    -19.739204499453752,
    64.93911745989001,
    -85.45013953080313,
    60.16763095037926,
    -25.96759924649648,
    6.5286581586731725,
)


def nn(a, b):
    return jnp.dot(a, b, preferred_element_type=F32)


def nt(a, b):
    return lax.dot_general(a, b, (((1,), (1,)), ((), ())), preferred_element_type=F32)


def split(x):
    high = x.astype(BF16)
    return high, (x - high.astype(F32)).astype(BF16)


def hot(mask):
    return jnp.where(mask, 1.0, 0.0).astype(BF16)


def iota(shape, dim):
    return lax.broadcasted_iota(I32, shape, dim)


def tn(a, b):
    return lax.dot_general(a, b, (((0,), (0,)), ((), ())), preferred_element_type=F32)


def sigmoid(x):
    return 0.5 * jnp.tanh(0.5 * x) + 0.5


def hot_rows(row, count):
    shape = (16, row.shape[1])
    named = jnp.broadcast_to(row, shape).astype(I16)
    index = iota(shape, 0).astype(I16)
    one, zero = jnp.ones(shape, BF16), jnp.zeros(shape, BF16)
    return jnp.concatenate([jnp.where(index + jnp.int16(i) == named, one, zero) for i in range(0, count, 16)], axis=0)


def cos_turns(y):
    r = y - jnp.floor(y + 0.5)
    z = r * r
    acc = jnp.full_like(z, COS[-1])
    for c in COS[-2::-1]:
        acc = acc * z + c
    return acc


def column(row):
    return jnp.broadcast_to(row, (LANES, LANES)).T


def partner(me, d):
    out = 0
    for bit in (1, 2, 4, 8, 16):
        out = out + lax.rem(lax.div(me, bit) + lax.div(d, bit), 2) * bit
    return out


def kernel(*refs):
    inputs, (new_mem_out, logits_out), held = refs[:15], refs[15:17], refs[17:32]
    mem, emb, own, rows, slots, ticks, w_self, w_neigh, w_time, w_link, w_score, w_msg, w_hid, freq, phase = held
    (
        new_mem, logits,
        hsend, hrecv, rsend, rmid, rrecv, esend, erecv, ssend, srecv, tsend, trecv, msend, mrecv,
        codes, csum, o_mat, g_mat, p_mat, c_mat,
        wg, wh, wp, base, time_part, self_acc, t_acc, s_acc,
        in_sem, out_sem, hsem, column_sem, ask_sem, send_sem, recv_sem,
    ) = refs[32:]
    me = lax.axis_index("mem")
    group = lax.axis_index("group")
    groups = lax.axis_size("group")
    ahead = lax.rem(group + 1, groups)
    behind = lax.rem(group + groups - 1, groups)
    width, events = 100, slots.shape[2]

    barrier = pltpu.get_barrier_semaphore()
    columns = (8, 16, 24)
    pl.semaphore_signal(barrier, inc=1, device_id={"group": behind}, device_id_type=MESH)
    for d in (1, 2, 3, 4, 5, 6, 7, *columns):
        pl.semaphore_signal(barrier, inc=1, device_id={"mem": partner(me, d)}, device_id_type=MESH)
    loads = [pltpu.make_async_copy(src, dst, in_sem.at[i]) for i, (src, dst) in enumerate(zip(inputs, held))]
    first, last = (2, 3, 0, 4, 5, 13, 14), (1, 6, 7, 8, 9, 10, 11, 12)
    for i in first + last:
        loads[i].start()

    def remote(phase_no, src, dst, d):
        return pltpu.make_async_remote_copy(
            src_ref=src.at[d],
            dst_ref=dst.at[d],
            send_sem=send_sem.at[phase_no, d],
            recv_sem=recv_sem.at[phase_no, d],
            device_id={"mem": partner(me, d)},
            device_id_type=MESH,
        )

    def start_all(phase_no, src, dst, which):
        for d in which:
            remote(phase_no, src, dst, d).start()

    def await_all(phase_no, src, dst, low, high):
        def go(d, c):
            remote(phase_no, src, dst, d).wait_recv()
            return c

        lax.fori_loop(low, high, go, 0)

    for i in first:
        loads[i].wait()
    for j in range(8):
        block = mem[pl.ds(j, width, stride=8), :]
        hsend[0:width, j * LANES : (j + 1) * LANES] = block.astype(BF16)
    hsend[96:112, :] = jnp.where(iota((16, 1024), 0) < 4, hsend[96:112, :].astype(F32), 0.0).astype(BF16)

    own_rel = own[...] ^ me
    local = rows[...]
    upper = iota((LANES, 2 * LANES), 0)
    lane = iota((LANES, 2 * LANES), 1)
    tri = hot((lane >= LANES) | (upper < lane))
    members = [jnp.where(iota((PEERS, LANES), 0) == own_rel[r : r + 1, :], 1.0, 0.0) for r in range(8)]
    counts = nn(jnp.concatenate(members, axis=0).astype(BF16), tri)
    seen = jnp.zeros((PEERS, LANES), F32)
    ranks = []
    for r in range(8):
        part = counts[r * PEERS : (r + 1) * PEERS, :]
        ranks.append(jnp.sum(members[r] * (part[:, :LANES] + seen), axis=0, keepdims=True))
        seen = seen + part[:, LANES:]
    rank_row = jnp.concatenate(ranks, axis=1)
    own_row = jnp.concatenate([own_rel[r : r + 1, :] for r in range(8)], axis=1)
    local_row = jnp.concatenate([local[r : r + 1, :] for r in range(8)], axis=1)
    rank_int = rank_row.astype(I32)
    in_rank = (iota((LANES, 1024), 0) & (CAP - 1)) == rank_int
    local_low = local_row & 31
    high_part = jnp.where(in_rank, (local_row - local_low).astype(F32), 0.0).astype(BF16)
    low_part = jnp.where(in_rank, local_low.astype(F32), 0.0).astype(BF16)
    member_row = hot_rows(own_row, PEERS)
    request = (nt(member_row, high_part) + nt(member_row, low_part)).astype(I32)
    for d in range(PEERS):
        rsend[d // 8, d % 8] = request[d : d + 1, :]
    rmid[0] = rsend[0]

    pl.semaphore_wait(barrier, 11)
    hand = pltpu.make_async_remote_copy(
        src_ref=hsend,
        dst_ref=hrecv.at[0:112],
        send_sem=hsem.at[0],
        recv_sem=hsem.at[1],
        device_id={"group": ahead},
        device_id_type=MESH,
    )
    hand.start()
    down = [
        pltpu.make_async_remote_copy(
            src_ref=rsend.at[d // 8],
            dst_ref=rmid.at[d // 8],
            send_sem=ask_sem.at[0, d // 8],
            recv_sem=ask_sem.at[1, d // 8],
            device_id={"mem": partner(me, d)},
            device_id_type=MESH,
        )
        for d in (16, 8, 24)
    ]
    for copy in down:
        copy.start()
    for d in columns:
        pl.semaphore_signal(column_sem, inc=1, device_id={"mem": partner(me, d)}, device_id_type=MESH)

    refs = jnp.concatenate([slots[0], slots[1]], axis=1)
    sub8 = iota((16, 1024), 0)
    slot_parts = jnp.where(sub8 == 0, own_row.astype(F32), jnp.where(sub8 == 1, rank_row, 0.0)).astype(BF16)
    picked = nn(slot_parts, hot_rows(refs, 1024))
    end_slot = (picked[0:1, :] * float(CAP) + picked[1:2, :]).astype(I32)
    g_mat[...] = hot_rows(end_slot, SLOTS)

    pad = jnp.zeros((1, LANES - width), F32)
    freq_col = column(jnp.concatenate([freq[...], pad], axis=1) * TURN)[0:104, :]
    phase_col = column(jnp.concatenate([phase[...], pad], axis=1) * TURN)[0:104, :]

    def code(k):
        tick = ticks[k].astype(F32)
        return jnp.concatenate(
            [cos_turns(freq_col * tick[:, h * LANES : (h + 1) * LANES] + phase_col) for h in range(events // LANES)],
            axis=1,
        )

    sub = iota((LANES, 2 * events), 0)
    side = iota((LANES, 2 * events), 1) // events
    ends = jnp.concatenate([code(0), code(1)], axis=1)
    ends = jnp.concatenate([ends, jnp.zeros((LANES - 104, 2 * events), F32)], axis=0)
    codes[...] = jnp.where(sub < width, ends, jnp.where(sub == width + side, 1.0, 0.0)).astype(BF16)

    sums = nt(g_mat[...], codes[...]).astype(BF16)
    for d in range(PEERS):
        tsend[d] = sums[d * CAP : (d + 1) * CAP, :]
    trecv[0] = tsend[0]
    for copy in down:
        copy.wait_recv()
    along = [
        pltpu.make_async_remote_copy(
            src_ref=rmid.at[:, d],
            dst_ref=rrecv.at[:, d],
            send_sem=ask_sem.at[2, d],
            recv_sem=ask_sem.at[3, d],
            device_id={"mem": partner(me, d)},
            device_id_type=MESH,
        )
        for d in (4, 5, 2, 3, 6, 7, 1)
    ]
    for copy in along:
        copy.start()
    for y in range(4):
        rrecv[y, 0] = rmid[y, 0]
    pl.semaphore_wait(column_sem, 3)
    start_all(1, tsend, trecv, FAR_FIRST)

    for copy in along:
        copy.wait_recv()
    for p in range(PEERS // 2):
        pair = jnp.where(iota((1, LANES), 1) < CAP, rrecv[p // 4, 2 * p % 8], rrecv[p // 4, 2 * p % 8 + 1])
        asked = column(pair.astype(F32)).astype(I32).astype(I16)
        for j in range(8):
            index = (iota((LANES, LANES), 1) + j * LANES).astype(I16)
            o_mat[p * LANES : (p + 1) * LANES, j * LANES : (j + 1) * LANES] = jnp.where(
                index == asked, jnp.ones((LANES, LANES), BF16), jnp.zeros((LANES, LANES), BF16)
            )
    def serve(rows_of, phase_no, src, dst):
        for q in Y_ORDER:
            got = nt(o_mat[q * 512 : (q + 1) * 512, :], rows_of[...]).astype(BF16)
            for i in range(8):
                src[q * 8 + i] = got[i * CAP : (i + 1) * CAP, :]
            start_all(phase_no, src, dst, [d for d in FAR_FIRST if d // 8 == q])
        dst[0] = src[0]

    def serve_embedding():
        loads[1].wait()
        serve(emb, 3, esend, erecv)

    @pl.when(group == 0)
    def _():
        serve_embedding()

    hand.wait_recv()
    hrecv[112:128, :] = jnp.zeros((16, 1024), BF16)
    serve(hrecv, 2, ssend, srecv)

    @pl.when(group != 0)
    def _():
        serve_embedding()

    for i in last[1:]:
        loads[i].wait()
    wg[...] = jnp.zeros_like(wg)
    wh[...] = jnp.zeros_like(wh)
    wp[...] = jnp.zeros_like(wp)
    for gate in range(3):
        for part in range(3):
            wg[part, gate * 112 : gate * 112 + width, 0:width] = w_msg[
                gate * width : (gate + 1) * width, part * width : (part + 1) * width
            ]
        wh[gate * 112 : gate * 112 + width, 0:width] = w_hid[gate * width : (gate + 1) * width, :]
    tally_lane = iota((16, LANES), 1)
    tally = (iota((16, LANES), 0) == 0) & ((tally_lane == width) | (tally_lane == width + 1))
    wg[2, 336:352, :] = hot(tally)
    for which, w in enumerate((w_self, w_neigh)):
        wp[which, 0:width, 0:width] = w[:, 0:width]
        wp[which, 0:width, LANES:] = w[:, width:]

    neighbours = (slots.shape[0] - 2) // 2
    one, zero = jnp.ones((16, 2 * events), BF16), jnp.zeros((16, 2 * events), BF16)
    index16 = iota((16, 2 * events), 0).astype(I16)
    near = [
        jnp.broadcast_to(jnp.concatenate([slots[2 + j], slots[2 + neighbours + j]], axis=1), one.shape).astype(I16)
        for j in range(neighbours)
    ]
    for q in range(64):
        total = zero
        index = index16 + jnp.int16(q * 16)
        for j in range(neighbours):
            total = total + jnp.where(index == near[j], one, zero)
        c_mat[q * 16 : (q + 1) * 16, :] = total
    p_mat[...] = hot_rows(own_row * CAP + rank_int, SLOTS)

    for s in range(2):
        def add_code(j, total, s=s):
            return total + code(2 + s * neighbours + j)

        csum[:, s * events : (s + 1) * events] = lax.fori_loop(
            0, neighbours, add_code, jnp.zeros((104, events), F32)
        )

    base[0:336, :] = nn(wg[0, 0:336, 0:112], hrecv[0:112, :])
    hidden = nn(wh[...], hrecv[0:112, :])
    base[0:224, :] = base[0:224, :] + hidden[0:224, :]
    base[336:448, :] = hidden[224:336, :]

    for q in Y_ORDER:
        await_all(2, ssend, srecv, max(q * 8, 1), q * 8 + 8)
        block = srecv[q * 8 : (q + 1) * 8].reshape(512, LANES)
        part = tn(block, g_mat[q * 512 : (q + 1) * 512, :])
        self_acc[...] = part if q == Y_ORDER[0] else self_acc[...] + part
    self_state = self_acc[...].astype(BF16)
    other_state = jnp.concatenate([self_state[:, events:], self_state[:, :events]], axis=1)
    for q in Y_ORDER:
        sums = nt(g_mat[q * 512 : (q + 1) * 512, :], other_state).astype(BF16)
        for i in range(8):
            msend[q * 8 + i] = sums[i * CAP : (i + 1) * CAP, :]
        start_all(4, msend, mrecv, [d for d in FAR_FIRST if d // 8 == q])
    mrecv[0] = msend[0]

    await_all(1, tsend, trecv, 1, PEERS)
    t_acc[...] = tn(trecv[...].reshape(SLOTS, LANES), o_mat[...]).astype(BF16)
    time_part[...] = nn(wg[2], t_acc[...])

    await_all(3, esend, erecv, 1, PEERS)
    embed_all = erecv[...].reshape(SLOTS, LANES)
    fetched_state = tn(srecv[...].reshape(SLOTS, LANES), p_mat[...]).astype(BF16)
    fetched_embed = tn(embed_all, p_mat[...]).astype(BF16)
    near_state = nn(fetched_state, c_mat[...])
    near_embed = nn(fetched_embed, c_mat[...])
    self_embed = tn(embed_all, g_mat[...]).astype(BF16)
    pre = nn(wp[0], jnp.concatenate([self_state, self_embed], axis=0))
    for half in split(jnp.concatenate([near_state, near_embed], axis=0)):
        pre = pre + nn(wp[1], half)
    high, low = split(csum[0:width, :])
    embeds = pre[0:width, :] + nn(w_time[...], high) + nn(w_time[...], low)
    embeds = jnp.maximum(embeds, 0.0).astype(BF16)
    link = tn(w_link[0:width, :], embeds[:, :events]) + tn(w_link[width:, :], embeds[:, events:])
    high, low = split(jnp.maximum(link, 0.0))
    score = jnp.broadcast_to(w_score[...], (16, width))
    logits[...] = (nn(score, high) + nn(score, low))[0:1, :].astype(BF16)

    score_out = pltpu.make_async_copy(logits, logits_out, out_sem.at[4])
    score_out.start()

    for q in Y_ORDER:
        await_all(4, msend, mrecv, max(q * 8, 1), q * 8 + 8)
        block = mrecv[q * 8 : (q + 1) * 8].reshape(512, LANES)
        part = tn(block, o_mat[q * 512 : (q + 1) * 512, :])
        s_acc[...] = part if q == Y_ORDER[0] else s_acc[...] + part

    outs = []
    for j in range(4):
        at = slice(j * 256, (j + 1) * 256)
        count = time_part[336:337, at]
        inverse = 1.0 / jnp.maximum(count, 1.0)
        total = (nn(wg[1, 0:336, :], s_acc[:, at].astype(BF16)) + time_part[0:336, at]) * inverse + base[0:336, at]
        reset = sigmoid(total[0:112])
        update = sigmoid(total[112:224])
        candidate = jnp.tanh(total[224:336] + reset * base[336:448, at])
        handed = hrecv[0:112, at].astype(F32)
        updated = candidate + update * (handed - candidate)
        new_mem[:, at] = jnp.where(count > 0.0, updated, handed)[0:width, :].astype(BF16)
        outs.append(pltpu.make_async_copy(new_mem.at[:, at], new_mem_out.at[:, at], out_sem.at[j]))
        outs[j].start()

    hand.wait_send()
    for copy in down + along:
        copy.wait_send()

    def drain(d, c):
        for phase_no, src, dst in (
            (1, tsend, trecv), (2, ssend, srecv), (3, esend, erecv), (4, msend, mrecv),
        ):
            remote(phase_no, src, dst, d).wait_send()
        return c

    lax.fori_loop(1, PEERS, drain, 0)
    score_out.wait()
    for copy in outs:
        copy.wait()


def hand_out(new_mem_in, logits_in, new_mem, logits):
    new_mem[...] = new_mem_in[...]
    logits[...] = logits_in[...]


def local_step(
    memory, embedding, owners, local_rows, event_slots, event_ticks,
    w_self, w_neighbour, w_time, w_link, w_score, w_message, w_hidden, frequencies, phases,
):
    nodes = memory.shape[2]
    events = event_slots.shape[2]
    args = (
        memory.reshape(-1, LANES),
        embedding,
        owners.reshape(-1, LANES),
        local_rows.reshape(-1, LANES),
        event_slots.transpose(1, 0, 2),
        event_ticks.transpose(1, 0, 2),
        w_self,
        w_neighbour,
        w_time,
        w_link.T,
        w_score.reshape(1, -1),
        w_message,
        w_hidden,
        frequencies.reshape(1, -1),
        phases.reshape(1, -1),
    )
    vmem = pl.BlockSpec(memory_space=pltpu.VMEM)
    hbm = pl.BlockSpec(memory_space=pl.ANY)
    block = (PEERS, CAP, LANES)
    scratch = [
        *[pltpu.VMEM(x.shape, x.dtype) for x in args],
        pltpu.VMEM((memory.shape[1], nodes), BF16),
        pltpu.VMEM((1, events), BF16),
        pltpu.VMEM((112, nodes), BF16),
        pltpu.VMEM((LANES, nodes), BF16),
        *[pltpu.VMEM((4, 8, 1, LANES), I32)] * 3,
        *[pltpu.VMEM(block, BF16)] * 8,
        pltpu.VMEM((LANES, 2 * events), BF16),
        pltpu.VMEM((104, 2 * events), F32),
        pltpu.VMEM((SLOTS, nodes), BF16),
        pltpu.VMEM((SLOTS, 2 * events), BF16),
        pltpu.VMEM((SLOTS, nodes), BF16),
        pltpu.VMEM((nodes, 2 * events), BF16),
        pltpu.VMEM((3, 352, LANES), BF16),
        pltpu.VMEM((336, 112), BF16),
        pltpu.VMEM((2, 112, 2 * LANES), BF16),
        pltpu.VMEM((448, nodes), F32),
        pltpu.VMEM((352, nodes), F32),
        pltpu.VMEM((LANES, 2 * events), F32),
        pltpu.VMEM((LANES, nodes), BF16),
        pltpu.VMEM((LANES, nodes), F32),
        pltpu.SemaphoreType.DMA((15,)),
        pltpu.SemaphoreType.DMA((5,)),
        pltpu.SemaphoreType.DMA((2,)),
        pltpu.SemaphoreType.REGULAR,
        pltpu.SemaphoreType.DMA((4, 8)),
        pltpu.SemaphoreType.DMA((5, PEERS)),
        pltpu.SemaphoreType.DMA((5, PEERS)),
    ]
    new_memory, logits = pl.pallas_call(
        kernel,
        out_shape=(
            jax.ShapeDtypeStruct((memory.shape[1], nodes), BF16),
            jax.ShapeDtypeStruct((1, events), BF16),
        ),
        in_specs=[hbm] * len(args),
        out_specs=(hbm, hbm),
        scratch_shapes=scratch,
        compiler_params=pltpu.CompilerParams(
            collective_id=0, has_side_effects=True, vmem_limit_bytes=56 * 1024 * 1024
        ),
    )(*args)
    new_memory, logits = pl.pallas_call(
        hand_out,
        out_shape=(
            jax.ShapeDtypeStruct((memory.shape[1], nodes), BF16),
            jax.ShapeDtypeStruct((1, events), BF16),
        ),
        in_specs=[vmem, vmem],
        out_specs=(vmem, vmem),
    )(new_memory, logits)
    return new_memory[None], logits


def solution(mesh):
    return jax.shard_map(
        local_step,
        mesh=mesh,
        in_specs=(
            P("group", None, "mem"),
            P(None, "mem"),
            P("group", "mem", None),
            P("group", "mem"),
            P("group", None, "mem"),
            P("group", None, "mem"),
            P(),
            P(),
            P(),
            P(),
            P(),
            P(),
            P(),
            P(),
            P(),
        ),
        out_specs=(P("group", None, "mem"), P("group", "mem")),
        check_vma=False,
    )
```

```python
import jax
import jax.numpy as jnp
from jax import lax
from jax.experimental import pallas as pl
from jax.experimental.pallas import tpu as pltpu
from jax.sharding import PartitionSpec as P

MESH = pl.DeviceIdType.MESH
F32, BF16, I32, I16 = jnp.float32, jnp.bfloat16, jnp.int32, jnp.int16
PEERS, CAP, LANES = 32, 64, 128
Y_ORDER = (2, 1, 3, 0)
FAR_FIRST = [8 * y + x for y in Y_ORDER for x in (4, 5, 2, 3, 6, 7, 0, 1) if 8 * y + x > 0]
HALF = CAP // 2
ROWS = PEERS * HALF
TURN = 0.15915494309189535
COS = (
    0.9999999890590219,
    -19.739204499453752,
    64.93911745989001,
    -85.45013953080313,
    60.16763095037926,
    -25.96759924649648,
    6.5286581586731725,
)


def nn(a, b):
    return jnp.dot(a, b, preferred_element_type=F32)


def nt(a, b):
    return lax.dot_general(a, b, (((1,), (1,)), ((), ())), preferred_element_type=F32)


def split(x):
    high = x.astype(BF16)
    return high, (x - high.astype(F32)).astype(BF16)


def hot(mask):
    return jnp.where(mask, 1.0, 0.0).astype(BF16)


def iota(shape, dim):
    return lax.broadcasted_iota(I32, shape, dim)


def tn(a, b):
    return lax.dot_general(a, b, (((0,), (0,)), ((), ())), preferred_element_type=F32)


def sigmoid(x):
    return 0.5 * jnp.tanh(0.5 * x) + 0.5


def hot_rows(row, count):
    shape = (16, row.shape[1])
    named = jnp.broadcast_to(row, shape).astype(I16)
    index = iota(shape, 0).astype(I16)
    one, zero = jnp.ones(shape, BF16), jnp.zeros(shape, BF16)
    return jnp.concatenate([jnp.where(index + jnp.int16(i) == named, one, zero) for i in range(0, count, 16)], axis=0)


def swap(x):
    return jnp.concatenate([x[:, CAP:], x[:, :CAP]], axis=1)


def by_half(half, row):
    return jnp.concatenate([jnp.where(half == 0, row, -1), jnp.where(half == 1, row, -1)], axis=1)


def cos_turns(y):
    r = y - jnp.floor(y + 0.5)
    z = r * r
    acc = jnp.full_like(z, COS[-1])
    for c in COS[-2::-1]:
        acc = acc * z + c
    return acc


def column(row):
    return jnp.broadcast_to(row, (LANES, LANES)).T


def partner(me, d):
    out = 0
    for bit in (1, 2, 4, 8, 16):
        out = out + lax.rem(lax.div(me, bit) + lax.div(d, bit), 2) * bit
    return out


def kernel(*refs):
    inputs, (new_mem, logits), held = refs[:15], refs[15:17], refs[17:32]
    mem, emb, own, rows, slots, ticks, w_self, w_neigh, w_time, w_link, w_score, w_msg, w_hid, freq, phase = held
    (
        hsend, hrecv, rsend, rmid, rrecv, esend, erecv, tsend, trecv,
        asend, arecv, bsend, brecv, masend, marecv, mbsend, mbrecv,
        codes, csum, o_mat, g_mat, p_mat, c_mat,
        wg, wh, wp, base, time_part, self_acc, t_acc, s_acc,
        in_sem, hsem, column_sem, ask_sem, send_sem, recv_sem,
    ) = refs[32:]
    me = lax.axis_index("mem")
    group = lax.axis_index("group")
    groups = lax.axis_size("group")
    ahead = lax.rem(group + 1, groups)
    behind = lax.rem(group + groups - 1, groups)
    width, events = 100, slots.shape[2]

    loads = [pltpu.make_async_copy(src, dst, in_sem.at[i]) for i, (src, dst) in enumerate(zip(inputs, held))]
    first, last = (2, 3, 4, 5, 13, 14), (1, 6, 7, 8, 9, 10, 11, 12)
    loads[0].start()
    barrier = pltpu.get_barrier_semaphore()
    columns = (8, 16, 24)
    pl.semaphore_signal(barrier, inc=1, device_id={"group": behind}, device_id_type=MESH)
    for d in (1, 2, 3, 4, 5, 6, 7, *columns):
        pl.semaphore_signal(barrier, inc=1, device_id={"mem": partner(me, d)}, device_id_type=MESH)
    for i in first + last:
        loads[i].start()

    def remote(phase_no, src, dst, d):
        return pltpu.make_async_remote_copy(
            src_ref=src.at[d],
            dst_ref=dst.at[d],
            send_sem=send_sem.at[phase_no, d],
            recv_sem=recv_sem.at[phase_no, d],
            device_id={"mem": partner(me, d)},
            device_id_type=MESH,
        )

    def start_all(phase_no, src, dst, which):
        for d in which:
            remote(phase_no, src, dst, d).start()

    def await_all(phase_no, src, dst, low, high):
        def go(d, c):
            remote(phase_no, src, dst, d).wait_recv()
            return c

        lax.fori_loop(low, high, go, 0)

    loads[0].wait()
    for j in range(8):
        block = mem[pl.ds(j, width, stride=8), :]
        hsend[0:width, j * LANES : (j + 1) * LANES] = block.astype(BF16)
    hsend[96:112, :] = jnp.where(iota((16, 1024), 0) < 4, hsend[96:112, :].astype(F32), 0.0).astype(BF16)

    for i in first:
        loads[i].wait()
    own_rel = own[...] ^ me
    local = rows[...]
    upper = iota((LANES, 2 * LANES), 0)
    lane = iota((LANES, 2 * LANES), 1)
    tri = hot((lane >= LANES) | (upper < lane))
    members = [jnp.where(iota((PEERS, LANES), 0) == own_rel[r : r + 1, :], 1.0, 0.0) for r in range(8)]
    counts = nn(jnp.concatenate(members, axis=0).astype(BF16), tri)
    seen = jnp.zeros((PEERS, LANES), F32)
    ranks = []
    for r in range(8):
        part = counts[r * PEERS : (r + 1) * PEERS, :]
        ranks.append(jnp.sum(members[r] * (part[:, :LANES] + seen), axis=0, keepdims=True))
        seen = seen + part[:, LANES:]
    rank_row = jnp.concatenate(ranks, axis=1)
    own_row = jnp.concatenate([own_rel[r : r + 1, :] for r in range(8)], axis=1)
    local_row = jnp.concatenate([local[r : r + 1, :] for r in range(8)], axis=1)
    rank_int = rank_row.astype(I32)
    place = iota((2 * LANES, 1024), 0)
    in_rank = (place // LANES) * HALF + (place & (HALF - 1)) == rank_int
    local_low = local_row & 31
    high_part = jnp.where(in_rank, (local_row - local_low).astype(F32), 0.0).astype(BF16)
    low_part = jnp.where(in_rank, local_low.astype(F32), 0.0).astype(BF16)
    member_row = hot_rows(own_row, PEERS)
    request = (nt(member_row, high_part) + nt(member_row, low_part)).astype(I32)
    for d in range(PEERS):
        for h in range(2):
            rsend[d // 8, d % 8, h : h + 1, :] = request[d : d + 1, h * LANES : (h + 1) * LANES]
    rmid[0] = rsend[0]

    refs = jnp.concatenate([slots[0], slots[1]], axis=1)
    sub8 = iota((16, 1024), 0)
    slot_parts = jnp.where(sub8 == 0, own_row.astype(F32), jnp.where(sub8 == 1, rank_row, 0.0)).astype(BF16)
    picked = nn(slot_parts, hot_rows(refs, 1024))
    end_rank = picked[1:2, :].astype(I32)
    end_row = picked[0:1, :].astype(I32) * HALF + (end_rank & (HALF - 1))
    g_mat[...] = hot_rows(by_half(end_rank // HALF, end_row), ROWS)

    pad = jnp.zeros((1, LANES - width), F32)
    freq_col = column(jnp.concatenate([freq[...], pad], axis=1) * TURN)[0:104, :]
    phase_col = column(jnp.concatenate([phase[...], pad], axis=1) * TURN)[0:104, :]

    def code(k):
        tick = ticks[k].astype(F32)
        return jnp.concatenate(
            [cos_turns(freq_col * tick[:, h * LANES : (h + 1) * LANES] + phase_col) for h in range(events // LANES)],
            axis=1,
        )

    sub = iota((LANES, 2 * events), 0)
    side = iota((LANES, 2 * events), 1) // events
    ends = jnp.concatenate([code(0), code(1)], axis=1)
    ends = jnp.concatenate([ends, jnp.zeros((LANES - 104, 2 * events), F32)], axis=0)
    codes[...] = jnp.where(sub < width, ends, jnp.where(sub == width + side, 1.0, 0.0)).astype(BF16)

    for h in range(2):
        sums = nt(g_mat[:, h * 2 * events : (h + 1) * 2 * events], codes[...]).astype(BF16)
        for d in range(PEERS):
            tsend[d, h * HALF : (h + 1) * HALF] = sums[d * HALF : (d + 1) * HALF, :]
    trecv[0] = tsend[0]
    pl.semaphore_wait(barrier, 11)
    hand = pltpu.make_async_remote_copy(
        src_ref=hsend,
        dst_ref=hrecv.at[0:112],
        send_sem=hsem.at[0],
        recv_sem=hsem.at[1],
        device_id={"group": ahead},
        device_id_type=MESH,
    )
    hand.start()
    down = [
        pltpu.make_async_remote_copy(
            src_ref=rsend.at[d // 8],
            dst_ref=rmid.at[d // 8],
            send_sem=ask_sem.at[0, d // 8],
            recv_sem=ask_sem.at[1, d // 8],
            device_id={"mem": partner(me, d)},
            device_id_type=MESH,
        )
        for d in (16, 8, 24)
    ]
    for copy in down:
        copy.start()
    for d in columns:
        pl.semaphore_signal(column_sem, inc=1, device_id={"mem": partner(me, d)}, device_id_type=MESH)

    start_all(1, tsend, trecv, [d for d in FAR_FIRST if d < 8 or d in columns])
    for copy in down:
        copy.wait_recv()
    along = [
        pltpu.make_async_remote_copy(
            src_ref=rmid.at[:, d],
            dst_ref=rrecv.at[:, d],
            send_sem=ask_sem.at[2, d],
            recv_sem=ask_sem.at[3, d],
            device_id={"mem": partner(me, d)},
            device_id_type=MESH,
        )
        for d in (4, 5, 2, 3, 6, 7, 1)
    ]
    for copy in along:
        copy.start()
    for y in range(4):
        rrecv[y, 0] = rmid[y, 0]
    pl.semaphore_wait(column_sem, 3)
    start_all(1, tsend, trecv, [d for d in FAR_FIRST if d >= 8 and d not in columns])

    for copy in along:
        copy.wait_recv()
    quarter = iota((1, LANES), 1) // HALF
    for p in range(PEERS // 4):
        for h in range(2):
            four = [rrecv[(4 * p + i) // 8, (4 * p + i) % 8, h : h + 1, :] for i in range(4)]
            ask = jnp.where(
                quarter < 2, jnp.where(quarter == 0, four[0], four[1]), jnp.where(quarter == 2, four[2], four[3])
            )
            asked = column(ask.astype(F32)).astype(I32).astype(I16)
            for j in range(8):
                index = (iota((LANES, LANES), 1) + j * LANES).astype(I16)
                o_mat[p * LANES : (p + 1) * LANES, h * 1024 + j * LANES : h * 1024 + (j + 1) * LANES] = jnp.where(
                    index == asked, jnp.ones((LANES, LANES), BF16), jnp.zeros((LANES, LANES), BF16)
                )

    def near_first(q):
        return [d for d in FAR_FIRST if d // 8 == q]

    def picked_rows(q, rows_of):
        return [nt(o_mat[q * 256 : (q + 1) * 256, h * 1024 : (h + 1) * 1024], rows_of[...]) for h in range(2)]

    def serve_embedding():
        loads[1].wait()
        for q in Y_ORDER:
            for h, got in enumerate(picked_rows(q, emb)):
                for i in range(8):
                    esend[q * 8 + i, h * HALF : (h + 1) * HALF] = got[i * HALF : (i + 1) * HALF, :].astype(BF16)
            start_all(3, esend, erecv, near_first(q))
        erecv[0] = esend[0]

    @pl.when(group == 0)
    def _():
        serve_embedding()

    hand.wait_recv()
    hrecv[112:128, :] = jnp.zeros((16, 1024), BF16)
    left = iota((256, LANES), 1) < CAP
    for q in Y_ORDER:
        first_half, second_half = picked_rows(q, hrecv)
        low = jnp.where(left, first_half, swap(second_half)).astype(BF16)
        high = jnp.where(left, swap(first_half), second_half).astype(BF16)
        for i in range(8):
            asend[q * 8 + i] = low[i * HALF : (i + 1) * HALF, :]
            bsend[q * 8 + i] = high[i * HALF : (i + 1) * HALF, :]
        start_all(2, asend, arecv, near_first(q))
    start_all(5, bsend, brecv, FAR_FIRST)
    arecv[0] = asend[0]
    brecv[0] = bsend[0]

    @pl.when(group != 0)
    def _():
        serve_embedding()

    for i in last[1:]:
        loads[i].wait()
    wg[...] = jnp.zeros_like(wg)
    wh[...] = jnp.zeros_like(wh)
    wp[...] = jnp.zeros_like(wp)
    for gate in range(3):
        for part in range(3):
            wg[part, gate * 112 : gate * 112 + width, 0:width] = w_msg[
                gate * width : (gate + 1) * width, part * width : (part + 1) * width
            ]
        wh[gate * 112 : gate * 112 + width, 0:width] = w_hid[gate * width : (gate + 1) * width, :]
    tally_lane = iota((16, LANES), 1)
    tally = (iota((16, LANES), 0) == 0) & ((tally_lane == width) | (tally_lane == width + 1))
    wg[2, 336:352, :] = hot(tally)
    for which, w in enumerate((w_self, w_neigh)):
        wp[which, 0:width, 0:width] = w[:, 0:width]
        wp[which, 0:width, LANES:] = w[:, width:]

    neighbours = (slots.shape[0] - 2) // 2
    one, zero = jnp.ones((16, 2 * events), BF16), jnp.zeros((16, 2 * events), BF16)
    index16 = iota((16, 2 * events), 0).astype(I16)
    near = [
        jnp.broadcast_to(jnp.concatenate([slots[2 + j], slots[2 + neighbours + j]], axis=1), one.shape).astype(I16)
        for j in range(neighbours)
    ]
    for q in range(64):
        total = zero
        index = index16 + jnp.int16(q * 16)
        for j in range(neighbours):
            total = total + jnp.where(index == near[j], one, zero)
        c_mat[q * 16 : (q + 1) * 16, :] = total
    p_mat[...] = hot_rows(by_half(rank_int // HALF, own_row * HALF + (rank_int & (HALF - 1))), ROWS)

    for s in range(2):
        def add_code(j, total, s=s):
            return total + code(2 + s * neighbours + j)

        csum[:, s * events : (s + 1) * events] = lax.fori_loop(
            0, neighbours, add_code, jnp.zeros((104, events), F32)
        )

    base[0:336, :] = nn(wg[0, 0:336, 0:112], hrecv[0:112, :])
    hidden = nn(wh[...], hrecv[0:112, :])
    base[0:224, :] = base[0:224, :] + hidden[0:224, :]
    base[336:448, :] = hidden[224:336, :]

    await_all(1, tsend, trecv, 1, PEERS)
    t_acc[...] = sum(
        tn(trecv[:, h * HALF : (h + 1) * HALF, :].reshape(ROWS, LANES), o_mat[:, h * 1024 : (h + 1) * 1024])
        for h in range(2)
    ).astype(BF16)
    time_part[...] = nn(wg[2], t_acc[...])

    self_parts = []
    wide = 2 * events
    for got_no, sent_no, src, dst, out, back in (
        (2, 4, asend, arecv, masend, marecv),
        (5, 6, bsend, brecv, mbsend, mbrecv),
    ):
        for q in Y_ORDER:
            await_all(got_no, src, dst, max(q * 8, 1), q * 8 + 8)
            block = dst[q * 8 : (q + 1) * 8].reshape(256, LANES)
            part = tn(block, g_mat[q * 256 : (q + 1) * 256, :])
            self_acc[...] = part if q == Y_ORDER[0] else self_acc[...] + part
        own_part = (self_acc[0:CAP, 0:wide] + self_acc[CAP:LANES, wide:]).astype(BF16)
        self_parts.append(own_part)
        turned = jnp.concatenate([own_part[:, events:], own_part[:, :events]], axis=1)
        blank = jnp.zeros((CAP, wide), BF16)
        packed = jnp.concatenate(
            [jnp.concatenate([turned, blank], axis=1), jnp.concatenate([blank, turned], axis=1)], axis=0
        )
        for q in Y_ORDER:
            sums = nt(g_mat[q * 256 : (q + 1) * 256, :], packed).astype(BF16)
            for i in range(8):
                out[q * 8 + i] = sums[i * HALF : (i + 1) * HALF, :]
            start_all(sent_no, out, back, near_first(q))
        back[0] = out[0]
    self_state = jnp.concatenate(self_parts, axis=0)

    await_all(3, esend, erecv, 1, PEERS)
    left = iota((ROWS, LANES), 1) < CAP
    low, high = arecv[...].reshape(ROWS, LANES).astype(F32), brecv[...].reshape(ROWS, LANES).astype(F32)
    state_rows = jnp.where(left, low, swap(high)).astype(BF16), jnp.where(left, swap(low), high).astype(BF16)
    embed_rows = [erecv[:, h * HALF : (h + 1) * HALF, :].reshape(ROWS, LANES) for h in range(2)]
    spread = [p_mat[:, h * 1024 : (h + 1) * 1024] for h in range(2)]
    fetched_state = (tn(state_rows[0], spread[0]) + tn(state_rows[1], spread[1])).astype(BF16)
    fetched_embed = (tn(embed_rows[0], spread[0]) + tn(embed_rows[1], spread[1])).astype(BF16)
    near_state = nn(fetched_state, c_mat[...])
    near_embed = nn(fetched_embed, c_mat[...])
    self_embed = (tn(embed_rows[0], g_mat[:, :wide]) + tn(embed_rows[1], g_mat[:, wide:])).astype(BF16)
    pre = nn(wp[0], jnp.concatenate([self_state, self_embed], axis=0))
    for half in split(jnp.concatenate([near_state, near_embed], axis=0)):
        pre = pre + nn(wp[1], half)
    high, low = split(csum[0:width, :])
    embeds = pre[0:width, :] + nn(w_time[...], high) + nn(w_time[...], low)
    embeds = jnp.maximum(embeds, 0.0).astype(BF16)
    link = tn(w_link[0:width, :], embeds[:, :events]) + tn(w_link[width:, :], embeds[:, events:])
    high, low = split(jnp.maximum(link, 0.0))
    score = jnp.broadcast_to(w_score[...], (16, width))
    logits[...] = (nn(score, high) + nn(score, low))[0:1, :].astype(BF16)

    await_all(4, masend, marecv, 1, PEERS)
    total = tn(marecv[...].reshape(ROWS, LANES), o_mat[...])
    s_acc[0:CAP, :] = total[0:CAP, 0:1024] + total[CAP:LANES, 1024:2048]
    for q in Y_ORDER:
        await_all(6, mbsend, mbrecv, max(q * 8, 1), q * 8 + 8)
        block = mbrecv[q * 8 : (q + 1) * 8].reshape(256, LANES)
        part = tn(block, o_mat[q * 256 : (q + 1) * 256, :])
        part = part[0:CAP, 0:1024] + part[CAP:LANES, 1024:2048]
        s_acc[CAP:LANES, :] = part if q == Y_ORDER[0] else s_acc[CAP:LANES, :] + part

    for j in range(4):
        at = slice(j * 256, (j + 1) * 256)
        count = time_part[336:337, at]
        inverse = 1.0 / jnp.maximum(count, 1.0)
        total = (nn(wg[1, 0:336, :], s_acc[:, at].astype(BF16)) + time_part[0:336, at]) * inverse + base[0:336, at]
        reset = sigmoid(total[0:112])
        update = sigmoid(total[112:224])
        candidate = jnp.tanh(total[224:336] + reset * base[336:448, at])
        handed = hrecv[0:112, at].astype(F32)
        updated = candidate + update * (handed - candidate)
        new_mem[:, at] = jnp.where(count > 0.0, updated, handed)[0:width, :].astype(BF16)

    hand.wait_send()
    for copy in down + along:
        copy.wait_send()

    def drain(d, c):
        for phase_no, src, dst in (
            (1, tsend, trecv), (2, asend, arecv), (3, esend, erecv), (4, masend, marecv), (5, bsend, brecv),
            (6, mbsend, mbrecv),
        ):
            remote(phase_no, src, dst, d).wait_send()
        return c

    lax.fori_loop(1, PEERS, drain, 0)


def local_step(
    memory, embedding, owners, local_rows, event_slots, event_ticks,
    w_self, w_neighbour, w_time, w_link, w_score, w_message, w_hidden, frequencies, phases,
):
    nodes = memory.shape[2]
    events = event_slots.shape[2]
    args = (
        memory.reshape(-1, LANES),
        embedding,
        owners.reshape(-1, LANES),
        local_rows.reshape(-1, LANES),
        event_slots.transpose(1, 0, 2),
        event_ticks.transpose(1, 0, 2),
        w_self,
        w_neighbour,
        w_time,
        w_link.T,
        w_score.reshape(1, -1),
        w_message,
        w_hidden,
        frequencies.reshape(1, -1),
        phases.reshape(1, -1),
    )
    vmem = pl.BlockSpec(memory_space=pltpu.VMEM)
    hbm = pl.BlockSpec(memory_space=pl.ANY)
    scratch = [
        *[pltpu.VMEM(x.shape, x.dtype) for x in args],
        pltpu.VMEM((112, nodes), BF16),
        pltpu.VMEM((LANES, nodes), BF16),
        *[pltpu.VMEM((4, 8, 2, LANES), I32)] * 3,
        *[pltpu.VMEM((PEERS, CAP, LANES), BF16)] * 4,
        *[pltpu.VMEM((PEERS, HALF, LANES), BF16)] * 8,
        pltpu.VMEM((LANES, 2 * events), BF16),
        pltpu.VMEM((104, 2 * events), F32),
        pltpu.VMEM((ROWS, 2 * nodes), BF16),
        pltpu.VMEM((ROWS, 4 * events), BF16),
        pltpu.VMEM((ROWS, 2 * nodes), BF16),
        pltpu.VMEM((nodes, 2 * events), BF16),
        pltpu.VMEM((3, 352, LANES), BF16),
        pltpu.VMEM((336, 112), BF16),
        pltpu.VMEM((2, 112, 2 * LANES), BF16),
        pltpu.VMEM((448, nodes), F32),
        pltpu.VMEM((352, nodes), F32),
        pltpu.VMEM((LANES, 4 * events), F32),
        pltpu.VMEM((LANES, nodes), BF16),
        pltpu.VMEM((LANES, nodes), F32),
        pltpu.SemaphoreType.DMA((15,)),
        pltpu.SemaphoreType.DMA((2,)),
        pltpu.SemaphoreType.REGULAR,
        pltpu.SemaphoreType.DMA((4, 8)),
        pltpu.SemaphoreType.DMA((7, PEERS)),
        pltpu.SemaphoreType.DMA((7, PEERS)),
    ]
    new_memory, logits = pl.pallas_call(
        kernel,
        out_shape=(
            pltpu.VMEM((memory.shape[1], nodes), BF16),
            pltpu.VMEM((1, events), BF16),
        ),
        in_specs=[pl.BlockSpec(memory_space=pltpu.HBM)] * len(args),
        out_specs=(vmem, vmem),
        scratch_shapes=scratch,
        compiler_params=pltpu.CompilerParams(
            collective_id=0, has_side_effects=True, vmem_limit_bytes=56 * 1024 * 1024
        ),
    )(*args)
    return new_memory[None], logits


def solution(mesh):
    return jax.shard_map(
        local_step,
        mesh=mesh,
        in_specs=(
            P("group", None, "mem"),
            P(None, "mem"),
            P("group", "mem", None),
            P("group", "mem"),
            P("group", None, "mem"),
            P("group", None, "mem"),
            P(),
            P(),
            P(),
            P(),
            P(),
            P(),
            P(),
            P(),
            P(),
        ),
        out_specs=(P("group", None, "mem"), P("group", "mem")),
        check_vma=False,
    )
```
